32 devices in a mesh: fsdp: 4 (over y, x), seq: 8 (over z, core).
Axes of the slice: x: 2, y: 2, z: 4, core: 2. Of those that a mesh axis runs over, the one named last changes fastest.
Arguments:
- tokens: bfloat16 [4096, 1024], P(('fsdp', 'seq')), may hold values from -6 to 6
- condition: bfloat16 [4, 1024], P('fsdp'), may hold values from -6 to 6
- block_image: int32 [32], P('fsdp'), may hold values from 0 to 3, as said below
- cotangent: bfloat16 [4096, 1024], P(('fsdp', 'seq')), may hold values from -6 to 6
- modul_weight: float32 [1024, 6144], P(('fsdp', 'seq')), may hold values from -0.1875 to 0.1875
- qkv_weight: float32 [1024, 3072], P(('fsdp', 'seq')), may hold values from -0.1875 to 0.1875
- proj_weight: float32 [1024, 1024], P(('fsdp', 'seq')), may hold values from -0.75 to 0.75
- widen_weight: float32 [1024, 4096], P(('fsdp', 'seq')), may hold values from -0.1875 to 0.1875
- narrow_weight: float32 [4096, 1024], P(('fsdp', 'seq')), may hold values from -0.09375 to 0.09375
- bias_vector: float32 [14336], P(('fsdp', 'seq')), may hold values from -1.5 to 1.5
- modul_mean: float32 [1024, 6144], P(('fsdp', 'seq')), may hold values from -20 to 20
- qkv_mean: float32 [1024, 3072], P(('fsdp', 'seq')), may hold values from -20 to 20
- proj_mean: float32 [1024, 1024], P(('fsdp', 'seq')), may hold values from -20 to 20
- widen_mean: float32 [1024, 4096], P(('fsdp', 'seq')), may hold values from -20 to 20
- narrow_mean: float32 [4096, 1024], P(('fsdp', 'seq')), may hold values from -20 to 20
- bias_mean: float32 [14336], P(('fsdp', 'seq')), may hold values from -20 to 20
- modul_square: float32 [1024, 6144], P(('fsdp', 'seq')), may hold values from 53.248 to 212.992
- qkv_square: float32 [1024, 3072], P(('fsdp', 'seq')), may hold values from 53.248 to 212.992
- proj_square: float32 [1024, 1024], P(('fsdp', 'seq')), may hold values from 53.248 to 212.992
- widen_square: float32 [1024, 4096], P(('fsdp', 'seq')), may hold values from 53.248 to 212.992
- narrow_square: float32 [4096, 1024], P(('fsdp', 'seq')), may hold values from 53.248 to 212.992
- bias_square: float32 [14336], P(('fsdp', 'seq')), may hold values from 2048 to 8192
Outputs:
- block_output: bfloat16 [4096, 1024], P(('fsdp', 'seq'))
- tokens_grad: bfloat16 [4096, 1024], P(('fsdp', 'seq'))
- condition_grad: float32 [4, 1024], P('fsdp')
- modul_updated: float32 [1024, 6144], P(('fsdp', 'seq'))
- qkv_updated: float32 [1024, 3072], P(('fsdp', 'seq'))
- proj_updated: float32 [1024, 1024], P(('fsdp', 'seq'))
- widen_updated: float32 [1024, 4096], P(('fsdp', 'seq'))
- narrow_updated: float32 [4096, 1024], P(('fsdp', 'seq'))
- bias_updated: float32 [14336], P(('fsdp', 'seq'))
- modul_momentum: float32 [1024, 6144], P(('fsdp', 'seq'))
- qkv_momentum: float32 [1024, 3072], P(('fsdp', 'seq'))
- proj_momentum: float32 [1024, 1024], P(('fsdp', 'seq'))
- widen_momentum: float32 [1024, 4096], P(('fsdp', 'seq'))
- narrow_momentum: float32 [4096, 1024], P(('fsdp', 'seq'))
- bias_momentum: float32 [14336], P(('fsdp', 'seq'))
- modul_variance: float32 [1024, 6144], P(('fsdp', 'seq'))
- qkv_variance: float32 [1024, 3072], P(('fsdp', 'seq'))
- proj_variance: float32 [1024, 1024], P(('fsdp', 'seq'))
- widen_variance: float32 [1024, 4096], P(('fsdp', 'seq'))
- narrow_variance: float32 [4096, 1024], P(('fsdp', 'seq'))
- bias_variance: float32 [14336], P(('fsdp', 'seq'))
The draws below stay inside these ranges and needn't reach their ends.
Inputs may be any that keep to these rules, and one draw needn't show every extreme that they name: `block_image`: every image is named by exactly 8 entries; the blocks held by fsdp index f (entries f * 8 * 1 to (f + 1) * 8 - 1) name only images f * 1 to (f + 1) - 1.
All inputs are finite; a program needn't handle non-finite values.
Results may differ from the reference program's by a relative error of at most 0.017.
The reference program's roundings to bfloat16 on the way count: a program that leaves them out, or rounds other values in their place, can miss the bound.
Values may be sent and summed in bfloat16 or wider, within the bound.
No kernel may reach another device: no remote copies, remote signals or barrier semaphores. Data moves between devices by JAX's collectives and lax.ppermute only.
A program may use at most 256 MiB of HBM per device.

```python
import math
import jax
import jax.numpy as jnp
from jax import lax

D = 1024
HEADS = 16
HEAD = 64
FF = 4096
BLOCK = 128
SEQ_LEN = 1024
STEP = 10
BLK_DEV = 1
TOKENS = 4096
BLOCKS = 32
IMG_GRP = 1
IMAGES = 4
NBIAS = 14336
N_FSDP = 4
N_SEQ = 8


def draw_block_image(key, part):
    key = jax.random.fold_in(key, 11)
    slot_count = N_SEQ * BLK_DEV
    per_image = SEQ_LEN // BLOCK
    forced = jnp.array([0, N_SEQ // 2 * BLK_DEV, slot_count - 1], jnp.int32)

    def one_group(group_key):
        order_key, image_key = jax.random.split(group_key)
        scores = jax.random.permutation(order_key, slot_count).astype(jnp.int32) + 3
        scores = scores.at[forced].set(jnp.arange(3, dtype=jnp.int32))
        ordering = jnp.argsort(scores).astype(jnp.int32)
        rankings = jnp.zeros((slot_count,), jnp.int32).at[ordering].set(jnp.arange(slot_count, dtype=jnp.int32))
        chosen = jax.random.randint(image_key, (), 0, IMG_GRP).astype(jnp.int32)
        return (rankings // per_image + chosen) % IMG_GRP
    local_ids = jax.vmap(one_group)(jax.random.split(key, N_FSDP))
    offsets = jnp.arange(N_FSDP, dtype=jnp.int32)[:, None] * IMG_GRP
    return (local_ids + offsets).reshape(-1).astype(jnp.int32)


def steps_of(rng, shape, cuts, least, top_value):
    level = 1.0
    for dim, blocks in cuts:
        heights = jax.random.uniform(jax.random.fold_in(jax.random.fold_in(rng, 6), dim), (blocks,), jnp.float32, least / len(cuts), top_value / len(cuts))
        level = level * jnp.repeat(jnp.exp(heights), shape[dim] // blocks).reshape((-1,) + (1,) * (len(shape) - 1 - dim))
    return level


def normal_values(rng, shape, deviation, bound, shards=(), kind=jnp.bfloat16):
    values = jax.random.normal(rng, shape, jnp.float32) * deviation
    if len(shards) > 0:
        values = steps_of(rng, shape, shards, -0.22, 0.18) * values
    return jnp.clip(values, min=-bound, max=bound).astype(kind)


def setup_inputs(seed: int = 0) -> dict:
    seeds = jax.random.split(jax.random.key(seed), 23)
    tokens = normal_values(seeds[0], (TOKENS, D), 1.0, 6.0, ((0, 32),))
    condition = normal_values(seeds[1], (IMAGES, D), 1.0, 6.0, ((0, 4),))
    block_image = draw_block_image(jax.random.fold_in(seeds[22], 71), 0)
    cotangent = normal_values(seeds[3], (TOKENS, D), 1.0, 6.0, ((0, 32),))
    modul_weight = normal_values(seeds[4], (D, 6 * D), D ** -0.5, 0.1875, ((0, 32),), jnp.float32)
    qkv_weight = normal_values(seeds[5], (D, 3 * D), D ** -0.5, 0.1875, ((0, 32),), jnp.float32)
    proj_weight = normal_values(seeds[6], (D, D), (D // 16) ** -0.5, 0.75, ((0, 32),), jnp.float32)
    widen_weight = normal_values(seeds[7], (D, FF), D ** -0.5, 0.1875, ((0, 32),), jnp.float32)
    narrow_weight = normal_values(seeds[8], (FF, D), FF ** -0.5, 0.09375, ((0, 32),), jnp.float32)
    bias_vector = normal_values(seeds[9], (NBIAS,), 0.3, 1.5, ((0, 32),), jnp.float32)
    modul_mean = normal_values(seeds[10], (D, 6 * D), (0.056 * TOKENS ** 0.5), 20.0, ((0, 32),), jnp.float32)
    qkv_mean = normal_values(seeds[11], (D, 3 * D), (0.056 * TOKENS ** 0.5), 20.0, ((0, 32),), jnp.float32)
    proj_mean = normal_values(seeds[12], (D, D), (0.056 * TOKENS ** 0.5), 20.0, ((0, 32),), jnp.float32)
    widen_mean = normal_values(seeds[13], (D, FF), (0.056 * TOKENS ** 0.5), 20.0, ((0, 32),), jnp.float32)
    narrow_mean = normal_values(seeds[14], (FF, D), (0.056 * TOKENS ** 0.5), 20.0, ((0, 32),), jnp.float32)
    bias_mean = normal_values(seeds[15], (NBIAS,), (0.056 * TOKENS ** 0.5), 20.0, ((0, 32),), jnp.float32)
    modul_square = jnp.clip(jnp.exp(math.log(212.992) - 1.3862944 * jax.random.uniform(seeds[16], (D, 6 * D), jnp.float32) ** steps_of(seeds[16], (D, 6 * D), ((0, 32),), -0.2, 0.2)), 53.248, 212.992)
    qkv_square = jnp.clip(jnp.exp(math.log(212.992) - 1.3862944 * jax.random.uniform(seeds[17], (D, 3 * D), jnp.float32) ** steps_of(seeds[17], (D, 3 * D), ((0, 32),), -0.2, 0.2)), 53.248, 212.992)
    proj_square = jnp.clip(jnp.exp(math.log(212.992) - 1.3862944 * jax.random.uniform(seeds[18], (D, D), jnp.float32) ** steps_of(seeds[18], (D, D), ((0, 32),), -0.2, 0.2)), 53.248, 212.992)
    widen_square = jnp.clip(jnp.exp(math.log(212.992) - 1.3862944 * jax.random.uniform(seeds[19], (D, FF), jnp.float32) ** steps_of(seeds[19], (D, FF), ((0, 32),), -0.2, 0.2)), 53.248, 212.992)
    narrow_square = jnp.clip(jnp.exp(math.log(212.992) - 1.3862944 * jax.random.uniform(seeds[20], (FF, D), jnp.float32) ** steps_of(seeds[20], (FF, D), ((0, 32),), -0.2, 0.2)), 53.248, 212.992)
    bias_square = jnp.clip(jnp.exp(math.log(8192.0) - 1.3862944 * jax.random.uniform(seeds[21], (NBIAS,), jnp.float32) ** steps_of(seeds[21], (NBIAS,), ((0, 32),), -0.2, 0.2)), 2048.0, 8192.0)
    return {"tokens": tokens, "condition": condition, "block_image": block_image, "cotangent": cotangent, "modul_weight": modul_weight, "qkv_weight": qkv_weight, "proj_weight": proj_weight, "widen_weight": widen_weight, "narrow_weight": narrow_weight, "bias_vector": bias_vector, "modul_mean": modul_mean, "qkv_mean": qkv_mean, "proj_mean": proj_mean, "widen_mean": widen_mean, "narrow_mean": narrow_mean, "bias_mean": bias_mean, "modul_square": modul_square, "qkv_square": qkv_square, "proj_square": proj_square, "widen_square": widen_square, "narrow_square": narrow_square, "bias_square": bias_square}


@jax.custom_vjp
def low(v):
    return lax.optimization_barrier(v.astype(jnp.bfloat16)).astype(jnp.float32)

@jax.custom_vjp
def low_back(v):
    return v

def low_keep(v):
    return (low(v), None)

def low_pass(kept, grad):
    return (grad,)

def back_keep(v):
    return (v, None)

def back_low(kept, grad):
    return (low(grad),)
low.defvjp(low_keep, low_pass)
low_back.defvjp(back_keep, back_low)
norm_eps = 1e-06
beta_first = 0.9
beta_second = 0.95
adam_eps = 1e-08
decay_rate = 0.01

def matmul(left, right):
    return jnp.dot(left, right, precision=lax.Precision.HIGHEST)

def layer_norm(values):
    center = values - lax.optimization_barrier(jnp.mean(values, axis=-1, keepdims=True))
    spread = lax.optimization_barrier(jnp.mean(center * center, axis=-1, keepdims=True))
    return center * lax.rsqrt(spread + norm_eps)

def modulate(values, shift, scale):
    return layer_norm(values) * (1.0 + scale[:, None, :]) + shift[:, None, :]

def attend_image(image_rows):
    queries = image_rows[:, :D].reshape(SEQ_LEN, HEADS, HEAD)
    keys = image_rows[:, D:2 * D].reshape(SEQ_LEN, HEADS, HEAD)
    values = image_rows[:, 2 * D:].reshape(SEQ_LEN, HEADS, HEAD)
    scores = jnp.einsum('qhd,khd->hqk', queries, keys, precision=lax.Precision.HIGHEST) * HEAD ** (-0.5)
    scores = low_back(scores)
    probs = low(jax.nn.softmax(scores, axis=-1))
    attended = jnp.einsum('hqk,khd->qhd', probs, values, precision=lax.Precision.HIGHEST)
    return low_back(low(attended.reshape(SEQ_LEN, D)))

def adam_step(weight, grad, first, second, rate):
    first = beta_first * first + (1.0 - beta_first) * grad
    second = beta_second * second + (1.0 - beta_second) * grad * grad
    fix_first = 1.0 - beta_first ** STEP
    fix_second = 1.0 - beta_second ** STEP
    weight = weight - rate * (first / fix_first / (jnp.sqrt(second / fix_second) + adam_eps) + decay_rate * weight)
    return (weight, first, second)

def reference(tokens, condition, block_image, cotangent, modul_weight, qkv_weight, proj_weight, widen_weight, narrow_weight, bias_vector, modul_mean, qkv_mean, proj_mean, widen_mean, narrow_mean, bias_mean, modul_square, qkv_square, proj_square, widen_square, narrow_square, bias_square):
    ordering = jnp.argsort(block_image, stable=True).astype(jnp.int32)
    inverse = jnp.argsort(ordering, stable=True).astype(jnp.int32)

    def forward(inputs, cond_float, w_modul, w_qkv, w_proj, w_widen, w_narrow, biases):
        w_modul = low(w_modul)
        w_qkv = low(w_qkv)
        w_proj = low(w_proj)
        w_widen = low(w_widen)
        w_narrow = low(w_narrow)
        biases = low(biases)
        bias_mod = biases[:6 * D]
        bias_query = biases[6 * D:7 * D]
        bias_value = biases[7 * D:8 * D]
        bias_proj = biases[8 * D:9 * D]
        bias_widen = biases[9 * D:9 * D + FF]
        bias_narrow = biases[9 * D + FF:]
        cond_act = low(jax.nn.silu(cond_float))
        modulation = matmul(cond_act, w_modul) + bias_mod
        per_block = modulation[block_image]
        shift_a, scale_a, gate_a, shift_b, scale_b, gate_b = jnp.split(per_block, 6, axis=1)
        blocks = inputs.reshape(BLOCKS, BLOCK, D)
        normed_a = low(modulate(blocks, shift_a, scale_a)).reshape(TOKENS, D)
        qkv_bias = jnp.concatenate([bias_query, jnp.zeros((D,), jnp.float32), bias_value])
        qkv = low_back(low(matmul(normed_a, w_qkv) + qkv_bias))
        grouped = qkv.reshape(BLOCKS, BLOCK, 3 * D)[ordering].reshape(IMAGES, SEQ_LEN, 3 * D)
        attended = lax.map(jax.checkpoint(attend_image), grouped)
        attended = attended.reshape(BLOCKS, BLOCK, D)[inverse].reshape(TOKENS, D)
        branch_a = low_back(matmul(attended, w_proj) + bias_proj).reshape(BLOCKS, BLOCK, D)
        middle = blocks + gate_a[:, None, :] * branch_a
        normed_b = low(modulate(middle, shift_b, scale_b)).reshape(TOKENS, D)
        widened = low_back(matmul(normed_b, w_widen) + bias_widen)
        activated = low(jax.nn.gelu(widened, approximate=True))
        branch_b = low_back(matmul(activated, w_narrow) + bias_narrow).reshape(BLOCKS, BLOCK, D)
        return (middle + gate_b[:, None, :] * branch_b).reshape(TOKENS, D)
    result, pull = jax.vjp(forward, tokens.astype(jnp.float32), condition.astype(jnp.float32), modul_weight, qkv_weight, proj_weight, widen_weight, narrow_weight, bias_vector)
    grads = pull(cotangent.astype(jnp.float32))
    rate_wide = 2.0 / math.sqrt(D)
    modul_updated, modul_momentum, modul_variance = adam_step(modul_weight, grads[2], modul_mean, modul_square, rate_wide)
    qkv_updated, qkv_momentum, qkv_variance = adam_step(qkv_weight, grads[3], qkv_mean, qkv_square, rate_wide)
    proj_updated, proj_momentum, proj_variance = adam_step(proj_weight, grads[4], proj_mean, proj_square, 2.0 / math.sqrt(D // 16))
    widen_updated, widen_momentum, widen_variance = adam_step(widen_weight, grads[5], widen_mean, widen_square, rate_wide)
    narrow_updated, narrow_momentum, narrow_variance = adam_step(narrow_weight, grads[6], narrow_mean, narrow_square, 2.0 / math.sqrt(FF))
    bias_updated, bias_momentum, bias_variance = adam_step(bias_vector, grads[7], bias_mean, bias_square, 0.5)
    return (result.astype(jnp.bfloat16), grads[0].astype(jnp.bfloat16), grads[1], modul_updated, qkv_updated, proj_updated, widen_updated, narrow_updated, bias_updated, modul_momentum, qkv_momentum, proj_momentum, widen_momentum, narrow_momentum, bias_momentum, modul_variance, qkv_variance, proj_variance, widen_variance, narrow_variance, bias_variance)
```

```python
import math

import jax
import jax.numpy as jnp
from jax import lax
from jax.sharding import PartitionSpec as P

D = 1024
HEADS = 16
HEAD = 64
FF = 4096
BLOCK = 128
SEQ_LEN = 1024
STEP = 10

CORES = 2

norm_eps = 1e-06
beta_first = 0.9
beta_second = 0.95
adam_eps = 1e-08
decay_rate = 0.01

f32 = jnp.float32
bf16 = jnp.bfloat16


def adam_step(weight, grad, first, second, rate):
    first = beta_first * first + (1.0 - beta_first) * grad
    second = beta_second * second + (1.0 - beta_second) * grad * grad
    fix_first = 1.0 - beta_first**STEP
    fix_second = 1.0 - beta_second**STEP
    weight = weight - rate * (
        first / fix_first / (jnp.sqrt(second / fix_second) + adam_eps) + decay_rate * weight
    )
    return (weight, first, second)


def normalize(values):
    center = values - jnp.mean(values, axis=-1, keepdims=True)
    spread = jnp.mean(center * center, axis=-1, keepdims=True)
    scale = lax.rsqrt(spread + norm_eps)
    return center * scale, scale


def norm_back(grad, normed, scale):
    mean_g = jnp.mean(grad, axis=-1, keepdims=True)
    mean_gn = jnp.mean(grad * normed, axis=-1, keepdims=True)
    return (grad - mean_g - normed * mean_gn) * scale


def matmul(left, right):
    return jnp.dot(left, right, preferred_element_type=f32)


def column_sums(values):
    return jnp.sum(values.astype(f32), axis=0)


def tree_sum(parts):
    while len(parts) > 1:
        parts = [parts[i] + parts[i + 1] for i in range(0, len(parts), 2)]
    return parts[0]


def xor_take(values, mask):
    order = jnp.arange(values.shape[0], dtype=jnp.int32) ^ mask
    return jnp.take(values, order, axis=0, mode="clip")


def xor_parts(parts, mask):
    step = 1
    while step < len(parts):
        turned = (mask & step) != 0
        parts = [jnp.where(turned, parts[i ^ step], parts[i]) for i in range(len(parts))]
        step *= 2
    return parts


def make_shards(n_f, n_z):
    n_s = n_z * CORES
    n_g = n_f * n_s
    heads_dev = HEADS // n_s
    hd = heads_dev * HEAD
    ub = FF // n_g
    rows = D // n_g
    units = n_z * ub

    def swap(values, axis, size, k):
        if k == 0:
            return values
        return lax.ppermute(values, axis, [(i, i ^ k) for i in range(size)])

    def swap_f(values, k):
        return swap(values, "fsdp", n_f, k)

    def swap_z(values, k):
        return swap(values, "z", n_z, k)

    def swap_c(values):
        return swap(values, "core", CORES, 1)

    def all_z(values):
        return [swap_z(values, k) for k in range(n_z)]

    def all_f(values):
        return [swap_f(values, k) for k in range(n_f)]

    def swap_rows_seq(values):
        both = jnp.stack([values[:, 0], swap_c(values[:, 1])], axis=1)
        return jnp.stack([swap_z(both[k], k) for k in range(n_z)])

    def reduce_seq(values):
        values = values + swap_c(values)
        return tree_sum(all_z(values))

    def shards(
        tokens,
        condition,
        block_image,
        cotangent,
        modul_weight,
        qkv_weight,
        proj_weight,
        widen_weight,
        narrow_weight,
        bias_vector,
        modul_mean,
        qkv_mean,
        proj_mean,
        widen_mean,
        narrow_mean,
        bias_mean,
        modul_square,
        qkv_square,
        proj_square,
        widen_square,
        narrow_square,
        bias_square,
    ):
        images_group = condition.shape[0]
        tok_group = n_s * BLOCK
        head_scale = HEAD ** (-0.5)
        at_f = lax.axis_index("fsdp")
        at_z = lax.axis_index("z")
        at_c = lax.axis_index("core")
        at_s = at_z * CORES + at_c
        at_g = at_f * n_s + at_s
        first_core = at_c == 0
        local_ids = block_image - at_f * images_group

        def own_other(values, axis):
            zero = lax.index_in_dim(values, 0, axis, keepdims=False)
            one = lax.index_in_dim(values, 1, axis, keepdims=False)
            return jnp.where(first_core, zero, one), jnp.where(first_core, one, zero)

        width = bias_vector.shape[0]
        pad = -(-width // 1024) * 1024
        small = jnp.concatenate(
            [
                jnp.pad(bias_vector.astype(bf16), (0, pad - width)).reshape(-1, 128),
                condition.reshape(-1, 128),
            ]
        )
        small = lax.all_gather(small, ("fsdp", "z", "core"), axis=0, tiled=False)
        bias_all = small[:, : pad // 128].reshape(n_g, pad)[:, :width].reshape(-1).astype(f32)
        cond_all = small.reshape(n_f, n_s, -1, 128)[:, 0, pad // 128 :]
        cond_all = cond_all.reshape(n_f * images_group, D).astype(f32)
        bias_mod = bias_all[: 6 * D]
        bias_query = bias_all[6 * D : 7 * D].reshape(n_s, hd)
        bias_value = bias_all[7 * D : 8 * D].reshape(n_s, hd)
        bias_proj = bias_all[8 * D : 9 * D]
        bias_widen = bias_all[9 * D : 9 * D + FF].reshape(n_f, n_z, CORES, ub)
        bias_narrow = bias_all[9 * D + FF :]

        modul_low = modul_weight.astype(bf16)
        modul_rows = lax.all_gather(modul_low, "fsdp", axis=0, tiled=True)

        tokens_z = jnp.stack(all_z(tokens))
        tokens_group = jnp.stack([tokens_z, swap_c(tokens_z)], axis=1).reshape(n_s, BLOCK, D)

        qkv_low = qkv_weight.astype(bf16).reshape(rows, 3, n_s, hd)
        qkv_out = xor_take(qkv_low.transpose(2, 0, 1, 3), at_s).reshape(n_z, CORES, rows, 3 * hd)
        qkv_mine = swap_rows_seq(qkv_out).reshape(n_s, rows, 3 * hd)
        qkv_in = jnp.stack(all_f(qkv_mine)).reshape(n_g, rows, 3 * hd)
        qkv_full = xor_take(qkv_in, at_g).reshape(D, 3 * hd)

        proj_full = lax.all_gather(
            proj_weight.astype(bf16), ("fsdp", "z", "core"), axis=0, tiled=True
        )
        narrow_full = lax.all_gather(narrow_weight.astype(bf16), "z", axis=0, tiled=True)
        widen_low = widen_weight.astype(bf16).reshape(rows, n_f, n_z, CORES, ub)
        widen_out = widen_low.transpose(1, 3, 0, 2, 4).reshape(n_f * CORES, rows, units)
        widen_mine = lax.all_to_all(widen_out, ("fsdp", "core"), 0, 0)
        widen_in = lax.all_gather(widen_mine.reshape(-1, units), "z", axis=0, tiled=False)
        widen_full = (
            widen_in.reshape(n_z, n_f, CORES, rows, units).transpose(1, 0, 2, 3, 4).reshape(D, units)
        )

        cond_float = condition.astype(f32)
        cond_act = jax.nn.silu(cond_float).astype(bf16).reshape(images_group, n_f, n_s, rows)
        cond_rows = lax.dynamic_index_in_dim(cond_act, at_s, 2, keepdims=False)
        modul_part = matmul(cond_rows.reshape(images_group, n_f * rows), modul_rows)
        modulation = reduce_seq(modul_part) + bias_mod

        own_id = lax.dynamic_index_in_dim(local_ids, at_s, keepdims=False)
        image_pick = (own_id == jnp.arange(images_group, dtype=jnp.int32)).astype(f32)
        if images_group == 1:
            own_row = modulation[0]
            group_rows = modulation
        else:
            own_row = jnp.sum(image_pick[:, None] * modulation, axis=0)
            rel_ids = xor_take(local_ids, at_s)
            rel_pick = (
                rel_ids[:, None] == jnp.arange(images_group, dtype=jnp.int32)[None, :]
            ).astype(f32)
            group_rows = jnp.sum(rel_pick[:, :, None] * modulation[None, :, :], axis=1)
            arrange = jnp.argsort(rel_ids, stable=True)
            restore = jnp.argsort(arrange, stable=True)
        shift_a, scale_a, gate_a, shift_b, scale_b, gate_b = [
            own_row[i * D : (i + 1) * D] for i in range(6)
        ]

        def by_image(values):
            if images_group > 1:
                values = values.reshape(n_s, BLOCK, hd)[arrange]
            values = values.reshape(images_group, SEQ_LEN, heads_dev, HEAD)
            return values.transpose(0, 2, 1, 3)

        def by_block(values):
            values = values.transpose(0, 2, 1, 3).reshape(tok_group, hd)
            if images_group > 1:
                values = values.reshape(n_s, BLOCK, hd)[restore].reshape(tok_group, hd)
            return values

        normed_group, _ = normalize(tokens_group.astype(f32))
        h_a = (
            normed_group * (1.0 + group_rows[:, None, D : 2 * D]) + group_rows[:, None, :D]
        ).astype(bf16)
        h_a = h_a.reshape(tok_group, D)
        query_bias = lax.dynamic_index_in_dim(bias_query, at_s, keepdims=False)
        value_bias = lax.dynamic_index_in_dim(bias_value, at_s, keepdims=False)
        qkv_bias = jnp.concatenate([query_bias, jnp.zeros((hd,), f32), value_bias])
        qkv = (matmul(h_a, qkv_full) + qkv_bias).astype(bf16)
        queries = by_image(qkv[:, :hd])
        keys = by_image(qkv[:, hd : 2 * hd])
        values = by_image(qkv[:, 2 * hd :])
        scores = (
            jnp.einsum("ihqd,ihkd->ihqk", queries, keys, preferred_element_type=f32) * head_scale
        )
        log_total = jax.nn.logsumexp(scores, axis=-1, keepdims=True)
        probs = jnp.exp(scores - log_total)
        probs_low = probs.astype(bf16)
        attended = by_block(
            jnp.einsum("ihqk,ihkd->ihqd", probs_low, values, preferred_element_type=f32).astype(
                bf16
            )
        )
        att_in = swap_rows_seq(attended.reshape(n_z, CORES, BLOCK, hd)).reshape(n_s, BLOCK, hd)
        att_own = xor_take(att_in, at_s).transpose(1, 0, 2).reshape(BLOCK, D)

        branch_a = matmul(att_own, proj_full) + bias_proj
        inputs = tokens.astype(f32)
        middle = inputs + gate_a * branch_a
        normed_b, spread_b = normalize(middle)
        h_b_own = (normed_b * (1.0 + scale_b) + shift_b).astype(bf16)
        grad_out = cotangent.astype(f32)
        d_b_own = (gate_b * grad_out).astype(bf16)

        d_b_f = lax.all_gather(d_b_own, "fsdp", axis=0, tiled=False)
        d_b = jnp.stack([d_b_f, swap_c(d_b_f)], axis=1).reshape(-1, D)
        h_b_f = jnp.stack(xor_parts(all_f(h_b_own), at_f))
        h_b = jnp.stack([h_b_f, swap_c(h_b_f)], axis=1).reshape(-1, D)
        bias_units = lax.dynamic_index_in_dim(bias_widen, at_f, 0, keepdims=False)
        bias_units = lax.dynamic_index_in_dim(bias_units, at_c, 1, keepdims=False).reshape(units)
        widened = matmul(h_b, widen_full) + bias_units
        activated, gelu_pull = jax.vjp(lambda u: jax.nn.gelu(u, approximate=True), widened)
        activated = activated.astype(bf16)
        d_act = jnp.einsum("td,fd->tf", d_b, narrow_full, preferred_element_type=f32)
        d_wide = gelu_pull(d_act)[0].astype(bf16)
        d_hb_part = jnp.einsum("tf,df->td", d_wide, widen_full, preferred_element_type=f32)

        def join_cores(values):
            return values[:, 0] + swap_c(values[:, 1].astype(bf16)).astype(f32)

        d_hb_f = join_cores(d_hb_part.reshape(n_f, CORES, BLOCK, D))
        d_hb_rel = [
            lax.dynamic_index_in_dim(d_hb_f, at_f ^ k, keepdims=False) for k in range(n_f)
        ]
        d_hb = tree_sum(
            [d_hb_rel[0]]
            + [swap_f(d_hb_rel[k].astype(bf16), k).astype(f32) for k in range(1, n_f)]
        )
        branch_part = join_cores(matmul(activated, narrow_full).reshape(n_f, CORES, BLOCK, D))
        branch_b = (
            lax.psum_scatter(branch_part, "fsdp", scatter_dimension=0, tiled=False) + bias_narrow
        )
        block_output = (middle + gate_b * branch_b).astype(bf16)
        d_gate_b = jnp.sum(grad_out * branch_b, axis=0)
        grad_narrow = jnp.einsum("tf,td->fd", activated, d_b, preferred_element_type=f32)
        narrow_sum = lax.psum_scatter(grad_narrow, "z", scatter_dimension=0, tiled=True)
        grad_widen = jnp.einsum("td,tf->df", h_b, d_wide, preferred_element_type=f32)
        grad_widen = grad_widen.reshape(n_f, n_z, CORES * rows, units).transpose(1, 0, 2, 3)
        widen_mid = lax.psum_scatter(
            grad_widen.reshape(n_z, -1, units), "z", scatter_dimension=0, tiled=False
        )
        widen_back = lax.all_to_all(
            widen_mid.astype(bf16).reshape(n_f * CORES, rows, units), ("fsdp", "core"), 0, 0
        )
        widen_sum = widen_back.reshape(n_f, CORES, rows, n_z, ub).transpose(2, 0, 3, 1, 4)
        widen_sum = widen_sum.reshape(rows, FF).astype(f32)

        d_shift_b = jnp.sum(d_hb, axis=0)
        d_scale_b = jnp.sum(d_hb * normed_b, axis=0)
        d_middle = grad_out + norm_back(d_hb * (1.0 + scale_b), normed_b, spread_b)
        d_gate_a = jnp.sum(d_middle * branch_a, axis=0)
        d_a = (gate_a * d_middle).astype(bf16)
        d_att_own = jnp.einsum("te,de->td", d_a, proj_full, preferred_element_type=f32)
        d_att_own = d_att_own.astype(bf16).reshape(BLOCK, n_s, hd).transpose(1, 0, 2)
        d_att_out = xor_take(d_att_own, at_s).reshape(n_z, CORES, BLOCK, hd)
        d_att = by_image(swap_rows_seq(d_att_out).reshape(tok_group, hd))
        grad_proj = jnp.einsum("td,te->de", att_own, d_a, preferred_element_type=f32)
        proj_own, proj_other = own_other(grad_proj.reshape(n_f * n_z, CORES, rows, D), 1)
        proj_both = proj_own + swap_c(proj_other.astype(bf16)).astype(f32)
        proj_sum = lax.psum_scatter(
            proj_both.reshape(-1, D), ("fsdp", "z"), scatter_dimension=0, tiled=True
        )

        d_values = jnp.einsum("ihqk,ihqd->ihkd", probs_low, d_att, preferred_element_type=f32)
        d_probs = jnp.einsum("ihqd,ihkd->ihqk", d_att, values, preferred_element_type=f32)
        row_term = jnp.sum(probs * d_probs, axis=-1, keepdims=True)
        d_scores = (probs * (d_probs - row_term)).astype(bf16)
        d_queries = (
            jnp.einsum("ihqk,ihkd->ihqd", d_scores, keys, preferred_element_type=f32) * head_scale
        )
        d_keys = (
            jnp.einsum("ihqk,ihqd->ihkd", d_scores, queries, preferred_element_type=f32)
            * head_scale
        )
        d_qkv = jnp.concatenate(
            [by_block(part.astype(bf16)) for part in (d_queries, d_keys, d_values)], axis=1
        )
        d_ha_part = jnp.einsum("te,de->td", d_qkv, qkv_full, preferred_element_type=f32)
        d_ha_z = join_cores(d_ha_part.reshape(n_z, CORES, BLOCK, D))
        d_ha = tree_sum(
            [d_ha_z[0]] + [swap_z(d_ha_z[k].astype(bf16), k).astype(f32) for k in range(1, n_z)]
        )
        grad_qkv = jnp.einsum("td,te->de", h_a, d_qkv, preferred_element_type=f32)
        grad_qkv = xor_take(grad_qkv.reshape(n_g, rows, 3 * hd), at_g)
        grad_qkv = grad_qkv.reshape(n_f, n_s, rows, 3 * hd)
        qkv_mid = tree_sum(
            [grad_qkv[0]]
            + [swap_f(grad_qkv[k].astype(bf16), k).astype(f32) for k in range(1, n_f)]
        )
        qkv_back = swap_rows_seq(qkv_mid.reshape(n_z, CORES, rows, 3 * hd))
        qkv_sum = xor_take(qkv_back.reshape(n_s, rows, 3, hd), at_s)
        qkv_sum = qkv_sum.transpose(1, 2, 0, 3).reshape(rows, 3 * D)
        normed_a, spread_a = normalize(inputs)
        d_shift_a = jnp.sum(d_ha, axis=0)
        d_scale_a = jnp.sum(d_ha * normed_a, axis=0)
        tokens_grad = (
            d_middle + norm_back(d_ha * (1.0 + scale_a), normed_a, spread_a)
        ).astype(bf16)

        pick_f = (jnp.arange(n_f) == at_f).astype(f32)
        pick_c = (jnp.arange(CORES) == at_c).astype(f32)
        pick_s = (jnp.arange(n_s) == at_s).astype(f32)
        units_sum = column_sums(d_wide).reshape(n_z, ub)
        bias_g_widen = (
            pick_f[:, None, None, None] * pick_c[None, None, :, None] * units_sum[None, :, None, :]
        ).reshape(FF)
        heads_sum = column_sums(d_qkv)
        bias_g_query = (pick_s[:, None] * heads_sum[None, :hd]).reshape(D)
        bias_g_value = (pick_s[:, None] * heads_sum[None, 2 * hd :]).reshape(D)
        d_block = jnp.concatenate([d_shift_a, d_scale_a, d_gate_a, d_shift_b, d_scale_b, d_gate_b])
        per_image = (image_pick[:, None] * d_block[None, :]).reshape(-1)
        sums = reduce_seq(
            jnp.concatenate(
                [
                    per_image,
                    bias_g_query,
                    bias_g_value,
                    column_sums(d_a),
                    bias_g_widen,
                    column_sums(d_b_own),
                ]
            )
        )
        split = images_group * 6 * D
        whole = jnp.stack(xor_parts(all_f(sums), at_f))
        d_modulation = whole[:, :split].reshape(n_f * images_group, 6 * D)
        all_act = jax.nn.silu(cond_all).astype(bf16).astype(f32)
        act_cols = lax.dynamic_slice_in_dim(all_act, at_g * rows, rows, axis=1)
        modul_sum = sum(
            act_cols[i][:, None] * d_modulation[i][None, :] for i in range(n_f * images_group)
        )
        bias_grad = jnp.concatenate(
            [jnp.sum(d_modulation, axis=0), jnp.sum(whole[:, split:], axis=0)]
        )
        bias_sum = lax.dynamic_slice_in_dim(bias_grad, at_g * width, width)
        d_own = sums[:split].reshape(images_group, 6 * D)
        d_cond_rows = jnp.einsum(
            "im,dm->id",
            d_own,
            modul_rows.astype(f32),
            precision=lax.Precision.HIGHEST,
            preferred_element_type=f32,
        )
        d_cond_z = jnp.stack(all_z(d_cond_rows))
        d_cond = jnp.stack([d_cond_z, swap_c(d_cond_z)], axis=1)
        d_cond = xor_take(d_cond.reshape(n_s, images_group, n_f, rows), at_s)
        d_cond_act = d_cond.transpose(1, 2, 0, 3).reshape(images_group, D)
        silu_pull = jax.vjp(jax.nn.silu, cond_float)[1]
        condition_grad = silu_pull(d_cond_act)[0]

        rate_wide = 2.0 / math.sqrt(D)
        modul_new = adam_step(modul_weight, modul_sum, modul_mean, modul_square, rate_wide)
        qkv_new = adam_step(qkv_weight, qkv_sum, qkv_mean, qkv_square, rate_wide)
        proj_new = adam_step(
            proj_weight, proj_sum, proj_mean, proj_square, 2.0 / math.sqrt(D // 16)
        )
        widen_new = adam_step(widen_weight, widen_sum, widen_mean, widen_square, rate_wide)
        narrow_new = adam_step(
            narrow_weight, narrow_sum, narrow_mean, narrow_square, 2.0 / math.sqrt(FF)
        )
        bias_new = adam_step(bias_vector, bias_sum, bias_mean, bias_square, 0.5)
        news = (modul_new, qkv_new, proj_new, widen_new, narrow_new, bias_new)
        return (
            block_output,
            tokens_grad,
            condition_grad,
            *[new[0] for new in news],
            *[new[1] for new in news],
            *[new[2] for new in news],
        )

    return shards


def solution(mesh):
    n_f, n_s = mesh.shape["fsdp"], mesh.shape["seq"]
    n_z = n_s // CORES
    cores = jax.sharding.Mesh(mesh.devices.reshape(n_f, n_z, CORES), ("fsdp", "z", "core"))
    both = P(("fsdp", "z", "core"), None)
    flat = P(("fsdp", "z", "core"))
    params = (both, both, both, both, both, flat)
    return jax.shard_map(
        make_shards(n_f, n_z),
        mesh=cores,
        in_specs=(both, P("fsdp", None), P("fsdp"), both) + params * 3,
        out_specs=(both, both, P("fsdp", None)) + params * 3,
        check_vma=False,
    )
```

```python
import math

import jax
import jax.numpy as jnp
from jax import lax
from jax.sharding import PartitionSpec as P

D = 1024
HEADS = 16
HEAD = 64
FF = 4096
BLOCK = 128
SEQ_LEN = 1024
STEP = 10

CORES = 2

norm_eps = 1e-06
beta_first = 0.9
beta_second = 0.95
adam_eps = 1e-08
decay_rate = 0.01

f32 = jnp.float32
bf16 = jnp.bfloat16


def adam_step(weight, grad, first, second, rate):
    first = beta_first * first + (1.0 - beta_first) * grad
    second = beta_second * second + (1.0 - beta_second) * grad * grad
    fix_first = 1.0 - beta_first**STEP
    fix_second = 1.0 - beta_second**STEP
    weight = weight - rate * (
        first / fix_first / (jnp.sqrt(second / fix_second) + adam_eps) + decay_rate * weight
    )
    return (weight, first, second)


def normalize(values):
    center = values - jnp.mean(values, axis=-1, keepdims=True)
    spread = jnp.mean(center * center, axis=-1, keepdims=True)
    scale = lax.rsqrt(spread + norm_eps)
    return center * scale, scale


def norm_back(grad, normed, scale):
    mean_g = jnp.mean(grad, axis=-1, keepdims=True)
    mean_gn = jnp.mean(grad * normed, axis=-1, keepdims=True)
    return (grad - mean_g - normed * mean_gn) * scale


def matmul(left, right):
    return jnp.dot(left, right, preferred_element_type=f32)


def column_sums(values):
    return jnp.sum(values.astype(f32), axis=0)


def tree_sum(parts):
    while len(parts) > 1:
        parts = [parts[i] + parts[i + 1] for i in range(0, len(parts), 2)]
    return parts[0]


def xor_take(values, mask):
    order = jnp.arange(values.shape[0], dtype=jnp.int32) ^ mask
    return jnp.take(values, order, axis=0, mode="clip")


def xor_parts(parts, mask):
    step = 1
    while step < len(parts):
        turned = (mask & step) != 0
        parts = [jnp.where(turned, parts[i ^ step], parts[i]) for i in range(len(parts))]
        step *= 2
    return parts


def make_shards(n_f, n_z):
    n_s = n_z * CORES
    n_g = n_f * n_s
    heads_dev = HEADS // n_s
    hd = heads_dev * HEAD
    ub = FF // n_g
    rows = D // n_g
    units = n_z * ub

    def swap(values, axis, size, k):
        if k == 0:
            return values
        return lax.ppermute(values, axis, [(i, i ^ k) for i in range(size)])

    def swap_f(values, k):
        return swap(values, "fsdp", n_f, k)

    def swap_z(values, k):
        return swap(values, "z", n_z, k)

    def swap_c(values):
        return swap(values, "core", CORES, 1)

    def all_z(values):
        return [swap_z(values, k) for k in range(n_z)]

    def all_f(values):
        return [swap_f(values, k) for k in range(n_f)]

    def double(values, swap_with, size):
        values = values[None]
        step = 1
        while step < size:
            values = jnp.concatenate([values, swap_with(values, step)])
            step *= 2
        return values

    def shift(entries, swap_with):
        entries = list(entries)
        step = 1
        while step < len(entries):
            moved = [k for k in range(len(entries)) if k & step]
            came = swap_with(jnp.stack([entries[k] for k in moved]), step)
            for i, k in enumerate(moved):
                entries[k] = came[i]
            step *= 2
        return entries

    def halve(parts, swap_with):
        parts = list(parts)
        step = len(parts) // 2
        while step > 0:
            low = jnp.stack([parts[k + step] for k in range(step)]).astype(bf16)
            came = swap_with(low, step)
            parts = [parts[k] + came[k].astype(f32) for k in range(step)]
            step //= 2
        return parts[0]

    def reduce_seq(values):
        values = values + swap_c(values)
        step = 1
        while step < n_z:
            values = values + swap_z(values, step)
            step *= 2
        return values

    def after(value, *others):
        return lax.optimization_barrier((value,) + others)[0]

    def join_cores(values):
        return values[:, 0] + swap_c(values[:, 1].astype(bf16)).astype(f32)

    def add_parts(own, parts):
        return tree_sum([own] + [part.astype(f32) for part in parts])

    def shards(
        tokens,
        condition,
        block_image,
        cotangent,
        modul_weight,
        qkv_weight,
        proj_weight,
        widen_weight,
        narrow_weight,
        bias_vector,
        modul_mean,
        qkv_mean,
        proj_mean,
        widen_mean,
        narrow_mean,
        bias_mean,
        modul_square,
        qkv_square,
        proj_square,
        widen_square,
        narrow_square,
        bias_square,
    ):
        images_group = condition.shape[0]
        tok_group = n_s * BLOCK
        head_scale = HEAD ** (-0.5)
        at_f = lax.axis_index("fsdp")
        at_z = lax.axis_index("z")
        at_c = lax.axis_index("core")
        at_s = at_z * CORES + at_c
        at_g = at_f * n_s + at_s
        first_core = at_c == 0
        local_ids = block_image - at_f * images_group

        pick_f = (jnp.arange(n_f) == at_f).astype(f32)
        pick_c = (jnp.arange(CORES) == at_c).astype(f32)
        pick_s = (jnp.arange(n_s) == at_s).astype(f32)

        def by_core(zero, one):
            return jnp.where(first_core, zero, one), jnp.where(first_core, one, zero)

        def trade_cores(zeros, ones):
            pairs = [by_core(zero, one) for zero, one in zip(zeros, ones)]
            came = swap_c(jnp.stack([other for _, other in pairs]))
            return [by_core(own, came[i]) for i, (own, _) in enumerate(pairs)]

        def trade_seq(entries):
            pairs = trade_cores(entries[0::2], entries[1::2])
            pairs = xor_parts([jnp.stack(pair) for pair in pairs], at_z)
            pairs = xor_parts(shift(pairs, swap_z), at_z)
            return [pairs[i // 2][i % 2] for i in range(n_s)]

        def trade_mlp(entries):
            pairs = trade_cores(entries[0::2], entries[1::2])
            pairs = xor_parts([jnp.stack(pair) for pair in pairs], at_f)
            pairs = xor_parts(shift(pairs, swap_f), at_f)
            return [pairs[i // 2][i % 2] for i in range(n_f * CORES)]

        width = bias_vector.shape[0]
        modul_low = modul_weight.astype(bf16)
        modul_rows = double(modul_low, swap_f, n_f).reshape(n_f * rows, 6 * D)
        small = double(jnp.concatenate([condition.reshape(-1), bias_vector.astype(bf16)]), swap_f, n_f)
        cond_all = small[:, : images_group * D]
        cond_all = cond_all.reshape(n_f * images_group, D).astype(f32)
        bias_rows = jnp.stack(
            xor_parts([small[k, images_group * D :] for k in range(n_f)], at_f)
        )
        bias_placed = (bias_rows.astype(f32)[:, None, :] * pick_s[None, :, None]).reshape(-1)

        tokens_z = jnp.stack(all_z(tokens))
        tokens_group = jnp.stack([tokens_z, swap_c(tokens_z)], axis=1).reshape(n_s, BLOCK, D)

        qkv_low = qkv_weight.astype(bf16).reshape(rows, 3, n_s, hd)
        qkv_mine = trade_seq([qkv_low[:, :, i].reshape(rows, 3 * hd) for i in range(n_s)])
        qkv_mine = jnp.stack(qkv_mine)
        qkv_full = jnp.stack(xor_parts(all_f(qkv_mine), at_f)).reshape(D, 3 * hd)

        proj_full = lax.all_gather(
            proj_weight.astype(bf16), ("fsdp", "z", "core"), axis=0, tiled=True
        )

        cond_float = condition.astype(f32)
        cond_act = jax.nn.silu(cond_float).astype(bf16).reshape(images_group, n_f, n_s, rows)
        cond_rows = lax.dynamic_index_in_dim(cond_act, at_s, 2, keepdims=False)
        cond_rows = jnp.stack(xor_parts([cond_rows[:, k] for k in range(n_f)], at_f), axis=1)
        modul_part = matmul(cond_rows.reshape(images_group, n_f * rows), modul_rows)
        modul_part = (modul_part + bias_placed[: 6 * D]).reshape(-1)
        whole = reduce_seq(jnp.concatenate([modul_part, bias_placed[6 * D :]]))
        modulation = whole[: images_group * 6 * D].reshape(images_group, 6 * D)
        bias_all = whole[images_group * 6 * D :]
        bias_query = bias_all[:D].reshape(n_s, hd)
        bias_value = bias_all[D : 2 * D].reshape(n_s, hd)
        bias_proj = bias_all[2 * D : 3 * D]
        bias_widen = bias_all[3 * D : 3 * D + FF].reshape(n_f, n_z, CORES, ub)
        bias_narrow = bias_all[3 * D + FF :]

        widen_late = after(widen_weight, qkv_mine)
        widen_low = widen_late.astype(bf16).reshape(rows, n_f, n_z, CORES, ub)
        widen_mine = trade_mlp(
            [
                widen_low[:, i // CORES, :, i % CORES].reshape(rows, units)
                for i in range(n_f * CORES)
            ]
        )
        narrow_low = narrow_weight.astype(bf16)
        hidden = jnp.concatenate(
            widen_mine + [narrow_low[:, i : i + units] for i in range(0, D, units)]
        )
        split = n_f * CORES * rows
        hidden = lax.all_gather(hidden, "z", axis=0, tiled=False)
        widen_full = hidden[:, :split].reshape(n_z, n_f, CORES * rows, units)
        widen_full = widen_full.transpose(1, 0, 2, 3).reshape(D, units)
        narrow_full = hidden[:, split:].reshape(n_z, D // units, ub, units)
        narrow_full = narrow_full.transpose(0, 2, 1, 3).reshape(units, D)

        own_id = lax.dynamic_index_in_dim(local_ids, at_s, keepdims=False)
        image_pick = (own_id == jnp.arange(images_group, dtype=jnp.int32)).astype(f32)
        if images_group == 1:
            own_row = modulation[0]
            group_rows = modulation
        else:
            own_row = jnp.sum(image_pick[:, None] * modulation, axis=0)
            rel_ids = xor_take(local_ids, at_s)
            rel_pick = (
                rel_ids[:, None] == jnp.arange(images_group, dtype=jnp.int32)[None, :]
            ).astype(f32)
            group_rows = jnp.sum(rel_pick[:, :, None] * modulation[None, :, :], axis=1)
            arrange = jnp.argsort(rel_ids, stable=True)
            restore = jnp.argsort(arrange, stable=True)
        shift_a, scale_a, gate_a, shift_b, scale_b, gate_b = [
            own_row[i * D : (i + 1) * D] for i in range(6)
        ]

        def by_image(values):
            if images_group > 1:
                values = values.reshape(n_s, BLOCK, hd)[arrange]
            values = values.reshape(images_group, SEQ_LEN, heads_dev, HEAD)
            return values.transpose(0, 2, 1, 3)

        def by_block(values):
            values = values.transpose(0, 2, 1, 3).reshape(tok_group, hd)
            if images_group > 1:
                values = values.reshape(n_s, BLOCK, hd)[restore].reshape(tok_group, hd)
            return values

        def send_blocks(values):
            came = swap_c(values[:, 1])
            parts = shift([jnp.stack([values[k, 0], came[k]]) for k in range(n_z)], swap_z)
            pairs = [by_core(part[0], part[1]) for part in xor_parts(parts, at_z)]
            return jnp.concatenate([part for pair in pairs for part in pair], axis=1)

        def send_heads(values):
            parts = [values[:, i * hd : (i + 1) * hd] for i in range(n_s)]
            pairs = [by_core(parts[2 * i], parts[2 * i + 1]) for i in range(n_z)]
            own = xor_parts([pair[0] for pair in pairs], at_z)
            other = xor_parts([pair[1] for pair in pairs], at_z)
            came = swap_c(jnp.stack(other))
            parts = shift([jnp.stack([own[k], came[k]]) for k in range(n_z)], swap_z)
            return jnp.stack(parts).reshape(tok_group, hd)

        normed_group, _ = normalize(tokens_group.astype(f32))
        h_a = (
            normed_group * (1.0 + group_rows[:, None, D : 2 * D]) + group_rows[:, None, :D]
        ).astype(bf16)
        h_a = h_a.reshape(tok_group, D)
        query_bias = lax.dynamic_index_in_dim(bias_query, at_s, keepdims=False)
        value_bias = lax.dynamic_index_in_dim(bias_value, at_s, keepdims=False)
        qkv_bias = jnp.concatenate([query_bias, jnp.zeros((hd,), f32), value_bias])
        qkv = (matmul(h_a, qkv_full) + qkv_bias).astype(bf16)
        queries = by_image(qkv[:, :hd])
        keys = by_image(qkv[:, hd : 2 * hd])
        values = by_image(qkv[:, 2 * hd :])
        scores = (
            jnp.einsum("ihqd,ihkd->ihqk", queries, keys, preferred_element_type=f32) * head_scale
        )
        log_total = jax.nn.logsumexp(scores, axis=-1, keepdims=True)
        probs = jnp.exp(scores - log_total)
        probs_low = probs.astype(bf16)
        attended = by_block(
            jnp.einsum("ihqk,ihkd->ihqd", probs_low, values, preferred_element_type=f32).astype(
                bf16
            )
        )
        att_own = send_blocks(attended.reshape(n_z, CORES, BLOCK, hd))

        branch_a = matmul(att_own, proj_full) + bias_proj
        inputs = tokens.astype(f32)
        middle = inputs + gate_a * branch_a
        normed_b, spread_b = normalize(middle)
        h_b_own = (normed_b * (1.0 + scale_b) + shift_b).astype(bf16)
        grad_out = cotangent.astype(f32)
        d_b_own = (gate_b * grad_out).astype(bf16)

        d_b_f = double(d_b_own, swap_f, n_f)
        d_b = jnp.stack([d_b_f, swap_c(d_b_f)], axis=1).reshape(-1, D)
        d_b = after(d_b, h_b_own)
        h_b_f = jnp.stack(all_f(h_b_own))
        h_b = jnp.stack([h_b_f, swap_c(h_b_f)], axis=1).reshape(-1, D)
        bias_units = lax.dynamic_index_in_dim(bias_widen, at_f, 0, keepdims=False)
        bias_units = lax.dynamic_index_in_dim(bias_units, at_c, 1, keepdims=False).reshape(units)
        widened = matmul(h_b, widen_full) + bias_units
        activated, gelu_pull = jax.vjp(lambda u: jax.nn.gelu(u, approximate=True), widened)
        activated = activated.astype(bf16)
        d_act = jnp.einsum("td,fd->tf", d_b, narrow_full, preferred_element_type=f32)
        d_wide = gelu_pull(d_act)[0].astype(bf16)
        d_hb_part = jnp.einsum("tf,df->td", d_wide, widen_full, preferred_element_type=f32)
        d_hb_f = join_cores(d_hb_part.reshape(n_f, CORES, BLOCK, D))
        d_hb = add_parts(d_hb_f[0], [swap_f(d_hb_f[k].astype(bf16), k) for k in range(1, n_f)])
        branch_part = join_cores(matmul(activated, narrow_full).reshape(n_f, CORES, BLOCK, D))
        grad_narrow = jnp.einsum("tf,td->fd", activated, d_b, preferred_element_type=f32)
        grad_widen = jnp.einsum("td,tf->df", h_b, d_wide, preferred_element_type=f32)
        grad_narrow = grad_narrow.reshape(n_z, ub, D)
        grad_widen = grad_widen.reshape(n_f, n_z, CORES, rows, units)

        grad_hidden = jnp.concatenate(
            [grad_widen.transpose(1, 0, 2, 3, 4).reshape(n_z, split, units)]
            + [grad_narrow[:, :, i : i + units] for i in range(0, D, units)],
            axis=1,
        )
        grad_hidden = after(grad_hidden.astype(bf16), d_hb_f)
        hidden_low = lax.psum_scatter(grad_hidden, "z", scatter_dimension=0, tiled=False)

        d_shift_b = jnp.sum(d_hb, axis=0)
        d_scale_b = jnp.sum(d_hb * normed_b, axis=0)
        d_middle = grad_out + norm_back(d_hb * (1.0 + scale_b), normed_b, spread_b)
        d_gate_a = jnp.sum(d_middle * branch_a, axis=0)
        d_a = (gate_a * d_middle).astype(bf16)
        d_att_own = jnp.einsum("te,de->td", d_a, proj_full, preferred_element_type=f32)
        d_att = by_image(send_heads(d_att_own.astype(bf16)))
        grad_proj = jnp.einsum("td,te->de", att_own, d_a, preferred_element_type=f32)
        grad_proj = grad_proj.reshape(n_f, n_z, CORES, rows, D)
        proj_own, proj_other = by_core(grad_proj[:, :, 0], grad_proj[:, :, 1])
        proj_both = proj_own + swap_c(proj_other.astype(bf16)).astype(f32)

        def mixed(k):
            part = lax.dynamic_index_in_dim(proj_both, at_f ^ k, 0, keepdims=False)
            return jnp.concatenate([branch_part[k], part.reshape(n_z * rows, D)])

        mixed_sum = halve([mixed(k) for k in range(n_f)], swap_f)

        d_values = jnp.einsum("ihqk,ihqd->ihkd", probs_low, d_att, preferred_element_type=f32)
        d_probs = jnp.einsum("ihqd,ihkd->ihqk", d_att, values, preferred_element_type=f32)
        row_term = jnp.sum(probs * d_probs, axis=-1, keepdims=True)
        d_scores = (probs * (d_probs - row_term)).astype(bf16)
        d_queries = (
            jnp.einsum("ihqk,ihkd->ihqd", d_scores, keys, preferred_element_type=f32) * head_scale
        )
        d_keys = (
            jnp.einsum("ihqk,ihqd->ihkd", d_scores, queries, preferred_element_type=f32)
            * head_scale
        )
        d_qkv = jnp.concatenate(
            [by_block(part.astype(bf16)) for part in (d_queries, d_keys, d_values)], axis=1
        )
        d_ha_part = jnp.einsum("te,de->td", d_qkv, qkv_full, preferred_element_type=f32)
        mixed_sum = after(mixed_sum, d_ha_part)
        branch_b = mixed_sum[:BLOCK] + bias_narrow
        block_output = (middle + gate_b * branch_b).astype(bf16)
        d_gate_b = jnp.sum(grad_out * branch_b, axis=0)
        proj_mid = xor_parts(
            [mixed_sum[i : i + rows] for i in range(BLOCK, BLOCK + n_z * rows, rows)], at_z
        )
        proj_sum = halve(proj_mid, swap_z)

        d_ha_z = join_cores(d_ha_part.reshape(n_z, CORES, BLOCK, D))
        d_ha = add_parts(d_ha_z[0], [swap_z(d_ha_z[k].astype(bf16), k) for k in range(1, n_z)])
        grad_qkv = jnp.einsum("td,te->de", h_a, d_qkv, preferred_element_type=f32)
        grad_qkv = grad_qkv.reshape(n_f, n_s * rows, 3 * hd)
        grad_qkv = [
            lax.dynamic_index_in_dim(grad_qkv, at_f ^ k, 0, keepdims=False) for k in range(n_f)
        ]
        qkv_mid = halve(grad_qkv, swap_f)
        qkv_sum = trade_seq([qkv_mid[i : i + rows] for i in range(0, n_s * rows, rows)])
        qkv_sum = jnp.stack(qkv_sum).reshape(n_s, rows, 3, hd)
        qkv_sum = qkv_sum.transpose(1, 2, 0, 3).reshape(rows, 3 * D)
        normed_a, spread_a = normalize(inputs)
        d_shift_a = jnp.sum(d_ha, axis=0)
        d_scale_a = jnp.sum(d_ha * normed_a, axis=0)
        tokens_grad = (
            d_middle + norm_back(d_ha * (1.0 + scale_a), normed_a, spread_a)
        ).astype(bf16)

        hidden_sum = after(hidden_low, d_ha).astype(f32)
        narrow_sum = jnp.concatenate(
            [hidden_sum[i : i + ub] for i in range(split, hidden_sum.shape[0], ub)], axis=1
        )
        widen_back = trade_mlp(
            [hidden_sum[i : i + rows].astype(bf16) for i in range(0, split, rows)]
        )
        widen_sum = jnp.stack(widen_back).reshape(n_f, CORES, rows, n_z, ub)
        widen_sum = widen_sum.transpose(2, 0, 3, 1, 4).reshape(rows, FF).astype(f32)

        units_sum = column_sums(d_wide).reshape(n_z, ub)
        bias_g_widen = (
            pick_f[:, None, None, None] * pick_c[None, None, :, None] * units_sum[None, :, None, :]
        ).reshape(FF)
        heads_sum = column_sums(d_qkv)
        bias_g_query = (pick_s[:, None] * heads_sum[None, :hd]).reshape(D)
        bias_g_value = (pick_s[:, None] * heads_sum[None, 2 * hd :]).reshape(D)
        d_block = jnp.concatenate([d_shift_a, d_scale_a, d_gate_a, d_shift_b, d_scale_b, d_gate_b])
        per_image = (image_pick[:, None] * d_block[None, :]).reshape(-1)
        pieces = [
            per_image,
            bias_g_query,
            bias_g_value,
            column_sums(d_a),
            bias_g_widen,
            column_sums(d_b_own),
        ]
        sums = reduce_seq(jnp.concatenate(pieces))
        cut = images_group * 6 * D
        whole = double(sums, swap_f, n_f)
        d_modulation = whole[:, :cut].reshape(n_f * images_group, 6 * D)
        all_act = jax.nn.silu(cond_all).astype(bf16).astype(f32)
        act_cols = lax.dynamic_slice_in_dim(all_act, at_g * rows, rows, axis=1)
        modul_sum = sum(
            act_cols[i][:, None] * d_modulation[i][None, :] for i in range(n_f * images_group)
        )
        bias_grad = jnp.concatenate(
            [jnp.sum(d_modulation, axis=0), jnp.sum(whole[:, cut:], axis=0)]
        )
        bias_sum = lax.dynamic_slice_in_dim(bias_grad, at_g * width, width)
        d_own = sums[:cut].reshape(images_group, 6 * D)
        d_cond_rows = jnp.einsum(
            "im,dm->id",
            d_own,
            modul_rows.astype(f32),
            precision=lax.Precision.HIGHEST,
            preferred_element_type=f32,
        )
        d_cond_z = double(d_cond_rows, swap_z, n_z)
        d_cond_z = jnp.stack(xor_parts([d_cond_z[k] for k in range(n_z)], at_z))
        d_cond = jnp.stack(by_core(d_cond_z, swap_c(d_cond_z)), axis=1)
        d_cond = d_cond.reshape(n_s, images_group, n_f, rows).transpose(2, 1, 0, 3)
        d_cond = jnp.stack(xor_parts([d_cond[k] for k in range(n_f)], at_f))
        d_cond_act = d_cond.transpose(1, 0, 2, 3).reshape(images_group, D)
        silu_pull = jax.vjp(jax.nn.silu, cond_float)[1]
        condition_grad = silu_pull(d_cond_act)[0]

        rate_wide = 2.0 / math.sqrt(D)
        modul_new = adam_step(modul_weight, modul_sum, modul_mean, modul_square, rate_wide)
        qkv_new = adam_step(qkv_weight, qkv_sum, qkv_mean, qkv_square, rate_wide)
        proj_new = adam_step(
            proj_weight, proj_sum, proj_mean, proj_square, 2.0 / math.sqrt(D // 16)
        )
        widen_new = adam_step(widen_weight, widen_sum, widen_mean, widen_square, rate_wide)
        narrow_new = adam_step(
            narrow_weight, narrow_sum, narrow_mean, narrow_square, 2.0 / math.sqrt(FF)
        )
        bias_new = adam_step(bias_vector, bias_sum, bias_mean, bias_square, 0.5)
        news = (modul_new, qkv_new, proj_new, widen_new, narrow_new, bias_new)
        return (
            block_output,
            tokens_grad,
            condition_grad,
            *[new[0] for new in news],
            *[new[1] for new in news],
            *[new[2] for new in news],
        )

    return shards


def solution(mesh):
    n_f, n_s = mesh.shape["fsdp"], mesh.shape["seq"]
    n_z = n_s // CORES
    cores = jax.sharding.Mesh(mesh.devices.reshape(n_f, n_z, CORES), ("fsdp", "z", "core"))
    both = P(("fsdp", "z", "core"), None)
    flat = P(("fsdp", "z", "core"))
    params = (both, both, both, both, both, flat)
    return jax.shard_map(
        make_shards(n_f, n_z),
        mesh=cores,
        in_specs=(both, P("fsdp", None), P("fsdp"), both) + params * 3,
        out_specs=(both, both, P("fsdp", None)) + params * 3,
        check_vma=False,
    )
```

```python
import math

import jax
import jax.numpy as jnp
from jax import lax
from jax.sharding import PartitionSpec as P

D = 1024
HEADS = 16
HEAD = 64
FF = 4096
BLOCK = 128
SEQ_LEN = 1024
STEP = 10

CORES = 2

norm_eps = 1e-06
beta_first = 0.9
beta_second = 0.95
adam_eps = 1e-08
decay_rate = 0.01

f32 = jnp.float32
bf16 = jnp.bfloat16


def adam_step(weight, grad, first, second, rate):
    first = beta_first * first + (1.0 - beta_first) * grad
    second = beta_second * second + (1.0 - beta_second) * grad * grad
    fix_first = 1.0 - beta_first**STEP
    fix_second = 1.0 - beta_second**STEP
    weight = weight - rate * (
        first / fix_first / (jnp.sqrt(second / fix_second) + adam_eps) + decay_rate * weight
    )
    return (weight, first, second)


def normalize(values):
    center = values - jnp.mean(values, axis=-1, keepdims=True)
    spread = jnp.mean(center * center, axis=-1, keepdims=True)
    scale = lax.rsqrt(spread + norm_eps)
    return center * scale, scale


def norm_back(grad, normed, scale):
    mean_g = jnp.mean(grad, axis=-1, keepdims=True)
    mean_gn = jnp.mean(grad * normed, axis=-1, keepdims=True)
    return (grad - mean_g - normed * mean_gn) * scale


def matmul(left, right):
    return jnp.dot(left, right, preferred_element_type=f32)


def column_sums(values):
    return jnp.sum(values.astype(f32), axis=0)


def tree_sum(parts):
    while len(parts) > 1:
        parts = [parts[i] + parts[i + 1] for i in range(0, len(parts), 2)]
    return parts[0]


def xor_take(values, mask):
    order = jnp.arange(values.shape[0], dtype=jnp.int32) ^ mask
    return jnp.take(values, order, axis=0, mode="clip")


def xor_parts(parts, mask):
    step = 1
    while step < len(parts):
        turned = (mask & step) != 0
        parts = [jnp.where(turned, parts[i ^ step], parts[i]) for i in range(len(parts))]
        step *= 2
    return parts


def make_shards(n_f, n_z):
    n_s = n_z * CORES
    n_g = n_f * n_s
    heads_dev = HEADS // n_s
    hd = heads_dev * HEAD
    ub = FF // n_g
    rows = D // n_g
    units = n_z * ub

    def swap(values, axis, size, k):
        if k == 0:
            return values
        return lax.ppermute(values, axis, [(i, i ^ k) for i in range(size)])

    def swap_f(values, k):
        return swap(values, "fsdp", n_f, k)

    def swap_z(values, k):
        return swap(values, "z", n_z, k)

    def swap_c(values):
        return swap(values, "core", CORES, 1)

    def all_z(values):
        return [swap_z(values, k) for k in range(n_z)]

    def all_f(values):
        return [swap_f(values, k) for k in range(n_f)]


    def run(*chains):
        results = [None] * len(chains)
        pending = {}
        for i, chain in enumerate(chains):
            try:
                pending[i] = next(chain)
            except StopIteration as stop:
                results[i] = stop.value
        while pending:
            leaves, tree = jax.tree.flatten(pending)
            if len(leaves) > 1:
                leaves = lax.optimization_barrier(leaves)
            came = jax.tree.unflatten(tree, leaves)
            pending = {}
            for i, value in came.items():
                try:
                    pending[i] = chains[i].send(value)
                except StopIteration as stop:
                    results[i] = stop.value
        return results

    def alone(chain):
        return run(chain)[0]

    def double(values, swap_with, size):
        values = values[None]
        step = 1
        while step < size:
            came = yield swap_with(values, step)
            values = jnp.concatenate([values, came])
            step *= 2
        return values

    def shift(entries, swap_with):
        entries = list(entries)
        step = 1
        while step < len(entries):
            moved = [k for k in range(len(entries)) if k & step]
            came = yield swap_with(jnp.stack([entries[k] for k in moved]), step)
            for i, k in enumerate(moved):
                entries[k] = came[i]
            step *= 2
        return entries

    def halve(parts, swap_with, kind=bf16):
        parts = list(parts)
        step = len(parts) // 2
        while step > 0:
            low = jnp.stack([parts[k + step] for k in range(step)]).astype(kind)
            came = yield swap_with(low, step)
            parts = [parts[k] + came[k].astype(f32) for k in range(step)]
            step //= 2
        return parts[0]

    def halve_near(parts, swap_with):
        parts = list(parts)
        step = 1
        while len(parts) > 1:
            low = jnp.stack(parts[1::2]).astype(bf16)
            came = yield swap_with(low, step)
            parts = [part + came[i].astype(f32) for i, part in enumerate(parts[0::2])]
            step *= 2
        return parts[0]

    def resume(chain, came, done=None):
        if came is None:
            return done
        try:
            came = chain.send(came)
        except StopIteration as stop:
            return stop.value
        while True:
            came = yield came
            try:
                came = chain.send(came)
            except StopIteration as stop:
                return stop.value

    def add_z(values):
        step = 1
        while step < n_z:
            came = yield swap_z(values, step)
            values = values + came
            step *= 2
        return values

    def add_seq(values):
        came = yield swap_c(values)
        values = yield from add_z(values + came)
        return values

    def after(value, *others):
        return lax.optimization_barrier((value,) + others)[0]

    def join_cores(values):
        low = values[:, 1].astype(bf16)
        return [
            values[k, 0] + swap_c(low[k]).astype(f32) for k in range(values.shape[0])
        ]

    def with_cores(pieces):
        return jnp.concatenate([part for own in pieces for part in (own, swap_c(own))])

    def add_parts(own, parts):
        return tree_sum([own] + [part.astype(f32) for part in parts])

    def shards(
        tokens,
        condition,
        block_image,
        cotangent,
        modul_weight,
        qkv_weight,
        proj_weight,
        widen_weight,
        narrow_weight,
        bias_vector,
        modul_mean,
        qkv_mean,
        proj_mean,
        widen_mean,
        narrow_mean,
        bias_mean,
        modul_square,
        qkv_square,
        proj_square,
        widen_square,
        narrow_square,
        bias_square,
    ):
        images_group = condition.shape[0]
        tok_group = n_s * BLOCK
        head_scale = HEAD ** (-0.5)
        at_f = lax.axis_index("fsdp")
        at_z = lax.axis_index("z")
        at_c = lax.axis_index("core")
        at_s = at_z * CORES + at_c
        at_g = at_f * n_s + at_s
        first_core = at_c == 0
        local_ids = block_image - at_f * images_group

        pick_f = (jnp.arange(n_f) == at_f).astype(f32)
        pick_c = (jnp.arange(CORES) == at_c).astype(f32)
        pick_s = (jnp.arange(n_s) == at_s).astype(f32)

        def by_core(zero, one):
            return jnp.where(first_core, zero, one), jnp.where(first_core, one, zero)

        def trade_cores(zeros, ones):
            pairs = [by_core(zero, one) for zero, one in zip(zeros, ones)]
            came = yield swap_c(jnp.stack([other for _, other in pairs]))
            return [by_core(own, came[i]) for i, (own, _) in enumerate(pairs)]

        def trade_seq(entries):
            pairs = yield from trade_cores(entries[0::2], entries[1::2])
            pairs = xor_parts([jnp.stack(pair) for pair in pairs], at_z)
            pairs = xor_parts((yield from shift(pairs, swap_z)), at_z)
            return [pairs[i // 2][i % 2] for i in range(n_s)]

        def trade_mlp(entries):
            pairs = yield from trade_cores(entries[0::2], entries[1::2])
            pairs = xor_parts([jnp.stack(pair) for pair in pairs], at_f)
            pairs = xor_parts((yield from shift(pairs, swap_f)), at_f)
            return [pairs[i // 2][i % 2] for i in range(n_f * CORES)]

        width = bias_vector.shape[0]
        modul_low = modul_weight.astype(bf16)
        tokens_z = all_z(tokens)
        tokens_group = with_cores(tokens_z).reshape(n_s, BLOCK, D)

        qkv_low = qkv_weight.astype(bf16).reshape(rows, 3, n_s, hd)

        proj_full = lax.all_gather(
            proj_weight.astype(bf16), ("fsdp", "z", "core"), axis=0, tiled=True
        )

        cond_float = condition.astype(f32)

        def modul_chain():
            small = yield from double(
                jnp.concatenate([condition.reshape(-1), bias_vector.astype(bf16)]), swap_f, n_f
            )
            cond_all = small[:, : images_group * D].reshape(n_f * images_group, D).astype(f32)
            all_act = jax.nn.silu(cond_all).astype(bf16)
            act_cols = lax.dynamic_slice_in_dim(all_act, at_g * rows, rows, axis=1)
            part = matmul(act_cols, modul_low).reshape(n_f, images_group, 6 * D)
            due = [part[k] for k in range(n_f)]
            while len(due) > 1:
                half = len(due) // 2
                low = jnp.stack(due[half:])
                if half == 1:
                    low = after(low, *tokens_z[1:])
                came = yield swap_f(low, half)
                due = [due[k] + came[k] for k in range(half)]
            part = due[0]
            bias_rows = xor_parts([small[k, images_group * D :] for k in range(n_f)], at_f)
            bias_rows = jnp.stack(bias_rows).astype(f32)
            placed = (bias_rows[:, None, :] * pick_s[None, :, None]).reshape(-1)
            part = (part + placed[: 6 * D]).reshape(-1)
            return act_cols, jnp.concatenate([part, placed[6 * D :]])

        widen_low = widen_weight.astype(bf16).reshape(rows, n_f, n_z, CORES, ub)
        (act_cols, whole), qkv_mine, widen_mine = run(
            modul_chain(),
            trade_seq([qkv_low[:, :, i].reshape(rows, 3 * hd) for i in range(n_s)]),
            trade_mlp(
                [
                    widen_low[:, i // CORES, :, i % CORES].reshape(rows, units)
                    for i in range(n_f * CORES)
                ]
            ),
        )
        qkv_parts = all_f(jnp.stack(qkv_mine))
        qkv_full = jnp.stack(xor_parts(qkv_parts, at_f)).reshape(D, 3 * hd)
        whole = whole + swap_c(whole)
        near = 1
        while near < n_z:
            if 2 * near == n_z:
                whole = after(whole, *qkv_parts[1:])
            whole = whole + swap_z(whole, near)
            near *= 2
        modulation = whole[: images_group * 6 * D].reshape(images_group, 6 * D)
        bias_all = whole[images_group * 6 * D :]
        bias_query = bias_all[:D].reshape(n_s, hd)
        bias_value = bias_all[D : 2 * D].reshape(n_s, hd)
        bias_proj = bias_all[2 * D : 3 * D]
        bias_widen = bias_all[3 * D : 3 * D + FF].reshape(n_f, n_z, CORES, ub)
        bias_narrow = bias_all[3 * D + FF :]

        widen_full = lax.all_gather(jnp.concatenate(widen_mine), "z", axis=0, tiled=False)
        widen_full = widen_full.reshape(n_z, n_f, CORES * rows, units)
        widen_full = widen_full.transpose(1, 0, 2, 3).reshape(D, units)
        narrow_late = after(narrow_weight, *widen_mine).astype(bf16)
        narrow_full = lax.all_gather(narrow_late, "z", axis=0, tiled=True)

        own_id = lax.dynamic_index_in_dim(local_ids, at_s, keepdims=False)
        image_pick = (own_id == jnp.arange(images_group, dtype=jnp.int32)).astype(f32)
        if images_group == 1:
            own_row = modulation[0]
            group_rows = modulation
        else:
            own_row = jnp.sum(image_pick[:, None] * modulation, axis=0)
            rel_ids = xor_take(local_ids, at_s)
            rel_pick = (
                rel_ids[:, None] == jnp.arange(images_group, dtype=jnp.int32)[None, :]
            ).astype(f32)
            group_rows = jnp.sum(rel_pick[:, :, None] * modulation[None, :, :], axis=1)
            arrange = jnp.argsort(rel_ids, stable=True)
            restore = jnp.argsort(arrange, stable=True)
        shift_a, scale_a, gate_a, shift_b, scale_b, gate_b = [
            own_row[i * D : (i + 1) * D] for i in range(6)
        ]

        def by_image(values):
            if images_group > 1:
                values = values.reshape(n_s, BLOCK, hd)[arrange]
            values = values.reshape(images_group, SEQ_LEN, heads_dev, HEAD)
            return values.transpose(0, 2, 1, 3)

        def by_block(values):
            values = values.transpose(0, 2, 1, 3).reshape(tok_group, hd)
            if images_group > 1:
                values = values.reshape(n_s, BLOCK, hd)[restore].reshape(tok_group, hd)
            return values

        def send_blocks(values):
            came = swap_c(values[:, 1])
            parts = [swap_z(jnp.stack([values[k, 0], came[k]]), k) for k in range(n_z)]
            pairs = [by_core(part[0], part[1]) for part in xor_parts(parts, at_z)]
            return jnp.concatenate([part for pair in pairs for part in pair], axis=1)

        def send_heads(values):
            parts = [values[:, i * hd : (i + 1) * hd] for i in range(n_s)]
            pairs = [by_core(parts[2 * i], parts[2 * i + 1]) for i in range(n_z)]
            own = xor_parts([pair[0] for pair in pairs], at_z)
            other = xor_parts([pair[1] for pair in pairs], at_z)
            came = swap_c(jnp.stack(other))
            parts = [swap_z(jnp.stack([own[k], came[k]]), k) for k in range(n_z)]
            return jnp.stack(parts).reshape(tok_group, hd)

        grad_out = cotangent.astype(f32)
        d_b_own = (gate_b * grad_out).astype(bf16)

        normed_group, _ = normalize(tokens_group.astype(f32))
        h_a = (
            normed_group * (1.0 + group_rows[:, None, D : 2 * D]) + group_rows[:, None, :D]
        ).astype(bf16)
        h_a = h_a.reshape(tok_group, D)
        query_bias = lax.dynamic_index_in_dim(bias_query, at_s, keepdims=False)
        value_bias = lax.dynamic_index_in_dim(bias_value, at_s, keepdims=False)
        qkv_bias = jnp.concatenate([query_bias, jnp.zeros((hd,), f32), value_bias])
        qkv = (matmul(h_a, qkv_full) + qkv_bias).astype(bf16)
        queries = by_image(qkv[:, :hd])
        keys = by_image(qkv[:, hd : 2 * hd])
        values = by_image(qkv[:, 2 * hd :])
        scores = (
            jnp.einsum("ihqd,ihkd->ihqk", queries, keys, preferred_element_type=f32) * head_scale
        )
        log_total = jax.nn.logsumexp(scores, axis=-1, keepdims=True)
        probs = jnp.exp(scores - log_total)
        probs_low = probs.astype(bf16)
        attended = by_block(
            jnp.einsum("ihqk,ihkd->ihqd", probs_low, values, preferred_element_type=f32).astype(
                bf16
            )
        )
        attended = after(attended, proj_full)
        att_own = send_blocks(attended.reshape(n_z, CORES, BLOCK, hd))

        branch_a = matmul(att_own, proj_full) + bias_proj
        inputs = tokens.astype(f32)
        middle = inputs + gate_a * branch_a
        normed_b, spread_b = normalize(middle)
        h_b_own = (normed_b * (1.0 + scale_b) + shift_b).astype(bf16)

        d_b_f = after(alone(double(d_b_own, swap_f, n_f)), h_b_own)
        modul_rows = lax.all_gather(after(modul_low, h_b_own), "fsdp", axis=0, tiled=True)
        d_b = with_cores([d_b_f[k] for k in range(n_f)])
        h_b = with_cores(all_f(h_b_own))
        bias_units = lax.dynamic_index_in_dim(bias_widen, at_f, 0, keepdims=False)
        bias_units = lax.dynamic_index_in_dim(bias_units, at_c, 1, keepdims=False).reshape(units)
        widened = matmul(h_b, widen_full) + bias_units
        activated, gelu_pull = jax.vjp(lambda u: jax.nn.gelu(u, approximate=True), widened)
        activated = activated.astype(bf16)
        d_act = jnp.einsum("td,fd->tf", d_b, narrow_full, preferred_element_type=f32)
        d_wide = gelu_pull(d_act)[0].astype(bf16)
        d_hb_part = jnp.einsum("tf,df->td", d_wide, widen_full, preferred_element_type=f32)
        d_hb_f = join_cores(d_hb_part.reshape(n_f, CORES, BLOCK, D))
        d_hb_came = [swap_f(d_hb_f[k].astype(bf16), k) for k in range(1, n_f)]
        grad_narrow = jnp.einsum("tf,td->fd", activated, d_b, preferred_element_type=f32)
        grad_narrow = after(grad_narrow, *d_hb_f).reshape(n_z, ub, D)
        narrow_chain = halve_near(
            [
                lax.dynamic_index_in_dim(grad_narrow, at_z ^ k, 0, keepdims=False)
                for k in range(n_z)
            ],
            swap_z,
        )
        narrow_came = next(narrow_chain)
        d_hb = add_parts(d_hb_f[0], [after(part, narrow_came) for part in d_hb_came])
        branch_part = matmul(activated, narrow_full).reshape(n_f, CORES, BLOCK, D)
        grad_widen = jnp.einsum("td,tf->df", h_b, d_wide, preferred_element_type=f32)
        grad_widen = grad_widen.astype(bf16).reshape(n_f, n_z, CORES, rows, units)
        grad_widen = grad_widen.transpose(1, 0, 2, 3, 4).reshape(n_z, -1, units)

        d_shift_b = jnp.sum(d_hb, axis=0)
        d_scale_b = jnp.sum(d_hb * normed_b, axis=0)
        d_middle = grad_out + norm_back(d_hb * (1.0 + scale_b), normed_b, spread_b)
        d_gate_a = jnp.sum(d_middle * branch_a, axis=0)
        d_a = (gate_a * d_middle).astype(bf16)
        d_att_own = jnp.einsum("te,de->td", d_a, proj_full, preferred_element_type=f32)
        d_att_own = d_att_own.astype(bf16)
        d_att = send_heads(d_att_own)
        grad_proj = jnp.einsum(
            "td,te->de", att_own, after(d_a, d_att_own), preferred_element_type=f32
        )
        grad_proj = grad_proj.reshape(n_f, n_z, CORES, rows, D)
        proj_own, proj_other = by_core(grad_proj[:, :, 0], grad_proj[:, :, 1])

        branch_chain = halve(join_cores(after(branch_part, d_hb)), swap_f)
        branch_came = next(branch_chain)

        def further(chain, came):
            try:
                return chain.send(came), None
            except StopIteration as stop:
                return None, stop.value

        narrow_came, narrow_sum = further(narrow_chain, narrow_came)
        if narrow_came is not None:
            d_att, narrow_came, branch_came = lax.optimization_barrier(
                (d_att, narrow_came, branch_came)
            )
        else:
            d_att, branch_came = lax.optimization_barrier((d_att, branch_came))
        branch_came, branch_b = further(branch_chain, branch_came)
        grad_widen = after(grad_widen, d_att)
        widen_part = lax.psum_scatter(grad_widen, "z", scatter_dimension=0, tiled=False)
        d_att = by_image(d_att)
        proj_both = proj_own + swap_c(proj_other.astype(bf16)).astype(f32)

        d_values = jnp.einsum("ihqk,ihqd->ihkd", probs_low, d_att, preferred_element_type=f32)
        d_probs = jnp.einsum("ihqd,ihkd->ihqk", d_att, values, preferred_element_type=f32)
        row_term = jnp.sum(probs * d_probs, axis=-1, keepdims=True)
        d_scores = (probs * (d_probs - row_term)).astype(bf16)
        d_queries = (
            jnp.einsum("ihqk,ihkd->ihqd", d_scores, keys, preferred_element_type=f32) * head_scale
        )
        d_keys = (
            jnp.einsum("ihqk,ihqd->ihkd", d_scores, queries, preferred_element_type=f32)
            * head_scale
        )
        d_qkv = jnp.concatenate(
            [by_block(part.astype(bf16)) for part in (d_queries, d_keys, d_values)], axis=1
        )
        if branch_came is not None:
            d_qkv, branch_came, proj_both = lax.optimization_barrier(
                (d_qkv, branch_came, proj_both)
            )
        else:
            d_qkv, proj_both = lax.optimization_barrier((d_qkv, proj_both))
        proj_chain = halve(
            [
                lax.dynamic_index_in_dim(proj_both, at_f ^ k, 0, keepdims=False)
                for k in range(n_f)
            ],
            swap_f,
        )
        d_ha_part = jnp.einsum("te,de->td", d_qkv, qkv_full, preferred_element_type=f32)
        d_ha_z = join_cores(d_ha_part.reshape(n_z, CORES, BLOCK, D))
        d_ha_low = [d_ha_z[k].astype(bf16) for k in range(1, n_z)]
        d_ha_came = [swap_z(d_ha_low[k - 1], k) for k in range(1, n_z)]
        grad_qkv = jnp.einsum("td,te->de", h_a, d_qkv, preferred_element_type=f32)
        grad_qkv = after(grad_qkv.reshape(n_f, n_s * rows, 3 * hd), *d_ha_low)
        grad_qkv = [
            lax.dynamic_index_in_dim(grad_qkv, at_f ^ k, 0, keepdims=False) for k in range(n_f)
        ]
        widen_part = after(widen_part, *d_ha_low).reshape(n_f * CORES, rows, units)

        branch_b, narrow_sum, proj_mid, qkv_mid, widen_back = run(
            resume(branch_chain, branch_came, branch_b),
            resume(narrow_chain, narrow_came, narrow_sum),
            proj_chain,
            halve(grad_qkv, swap_f),
            trade_mlp([widen_part[i] for i in range(n_f * CORES)]),
        )
        d_ha_came = [after(part, branch_b, proj_mid, qkv_mid, *widen_back) for part in d_ha_came]
        d_ha = add_parts(d_ha_z[0], d_ha_came)
        widen_sum = jnp.stack(widen_back).reshape(n_f, CORES, rows, n_z, ub)
        widen_sum = widen_sum.transpose(2, 0, 3, 1, 4).reshape(rows, FF).astype(f32)
        branch_b = branch_b + bias_narrow
        block_output = (middle + gate_b * branch_b).astype(bf16)
        d_gate_b = jnp.sum(grad_out * branch_b, axis=0)
        normed_a, spread_a = normalize(inputs)
        d_shift_a = jnp.sum(d_ha, axis=0)
        d_scale_a = jnp.sum(d_ha * normed_a, axis=0)
        tokens_grad = (
            d_middle + norm_back(d_ha * (1.0 + scale_a), normed_a, spread_a)
        ).astype(bf16)

        units_sum = column_sums(d_wide).reshape(n_z, ub)
        bias_g_widen = (
            pick_f[:, None, None, None] * pick_c[None, None, :, None] * units_sum[None, :, None, :]
        ).reshape(FF)
        heads_sum = column_sums(d_qkv)
        bias_g_query = (pick_s[:, None] * heads_sum[None, :hd]).reshape(D)
        bias_g_value = (pick_s[:, None] * heads_sum[None, 2 * hd :]).reshape(D)
        d_block = jnp.concatenate([d_shift_a, d_scale_a, d_gate_a, d_shift_b, d_scale_b, d_gate_b])
        per_image = (image_pick[:, None] * d_block[None, :]).reshape(-1)
        pieces = [
            per_image,
            bias_g_query,
            bias_g_value,
            column_sums(d_a),
            bias_g_widen,
            column_sums(d_b_own),
        ]
        sums = alone(add_seq(jnp.concatenate(pieces)))
        cut = images_group * 6 * D
        d_own = sums[:cut].reshape(images_group, 6 * D)
        d_cond_rows = jnp.einsum(
            "im,dm->id",
            d_own,
            modul_rows.astype(f32),
            precision=lax.Precision.HIGHEST,
            preferred_element_type=f32,
        )

        def cond_chain():
            part = yield from double(d_cond_rows, swap_z, n_z)
            part = jnp.stack(xor_parts([part[k] for k in range(n_z)], at_z))
            came = yield swap_c(part)
            return jnp.stack(by_core(part, came), axis=1)

        qkv_mid = after(qkv_mid, sums)
        proj_mid = after(proj_mid, sums)
        whole, d_cond, proj_sum, qkv_sum = run(
            double(sums, swap_f, n_f),
            cond_chain(),
            halve(xor_parts([proj_mid[k] for k in range(n_z)], at_z), swap_z),
            trade_seq([qkv_mid[i : i + rows] for i in range(0, n_s * rows, rows)]),
        )
        qkv_sum = jnp.stack(qkv_sum).reshape(n_s, rows, 3, hd)
        qkv_sum = qkv_sum.transpose(1, 2, 0, 3).reshape(rows, 3 * D)
        d_cond = d_cond.reshape(n_s, images_group, n_f, rows)
        d_cond_act = d_cond.transpose(1, 2, 0, 3).reshape(images_group, D)
        silu_pull = jax.vjp(jax.nn.silu, cond_float)[1]
        condition_grad = silu_pull(d_cond_act)[0]

        d_modulation = whole[:, :cut].reshape(n_f * images_group, 6 * D)
        act_wide = act_cols.astype(f32)
        modul_sum = sum(
            act_wide[i][:, None] * d_modulation[i][None, :] for i in range(n_f * images_group)
        )
        bias_grad = jnp.concatenate(
            [jnp.sum(d_modulation, axis=0), jnp.sum(whole[:, cut:], axis=0)]
        )
        bias_sum = lax.dynamic_slice_in_dim(bias_grad, at_g * width, width)

        rate_wide = 2.0 / math.sqrt(D)
        modul_new = adam_step(modul_weight, modul_sum, modul_mean, modul_square, rate_wide)
        qkv_new = adam_step(qkv_weight, qkv_sum, qkv_mean, qkv_square, rate_wide)
        proj_new = adam_step(
            proj_weight, proj_sum, proj_mean, proj_square, 2.0 / math.sqrt(D // 16)
        )
        widen_new = adam_step(widen_weight, widen_sum, widen_mean, widen_square, rate_wide)
        narrow_new = adam_step(
            narrow_weight, narrow_sum, narrow_mean, narrow_square, 2.0 / math.sqrt(FF)
        )
        bias_new = adam_step(bias_vector, bias_sum, bias_mean, bias_square, 0.5)
        news = (modul_new, qkv_new, proj_new, widen_new, narrow_new, bias_new)
        return (
            block_output,
            tokens_grad,
            condition_grad,
            *[new[0] for new in news],
            *[new[1] for new in news],
            *[new[2] for new in news],
        )

    return shards


def solution(mesh):
    n_f, n_s = mesh.shape["fsdp"], mesh.shape["seq"]
    n_z = n_s // CORES
    cores = jax.sharding.Mesh(mesh.devices.reshape(n_f, n_z, CORES), ("fsdp", "z", "core"))
    both = P(("fsdp", "z", "core"), None)
    flat = P(("fsdp", "z", "core"))
    params = (both, both, both, both, both, flat)
    return jax.shard_map(
        make_shards(n_f, n_z),
        mesh=cores,
        in_specs=(both, P("fsdp", None), P("fsdp"), both) + params * 3,
        out_specs=(both, both, P("fsdp", None)) + params * 3,
        check_vma=False,
    )
```

```python
import math

import jax
import jax.numpy as jnp
from jax import lax
from jax.experimental import pallas as pl
from jax.experimental.pallas import tpu as pltpu
from jax.sharding import PartitionSpec as P

D = 1024
HEADS = 16
HEAD = 64
FF = 4096
BLOCK = 128
SEQ_LEN = 1024
STEP = 10

CORES = 2
QUERIES = 256

norm_eps = 1e-06
beta_first = 0.9
beta_second = 0.95
adam_eps = 1e-08
decay_rate = 0.01

f32 = jnp.float32
bf16 = jnp.bfloat16


def adam_step(weight, grad, first, second, rate):
    first = beta_first * first + (1.0 - beta_first) * grad
    second = beta_second * second + (1.0 - beta_second) * grad * grad
    fix_first = 1.0 - beta_first**STEP
    fix_second = 1.0 - beta_second**STEP
    weight = weight - rate * (
        first / fix_first / (jnp.sqrt(second / fix_second) + adam_eps) + decay_rate * weight
    )
    return (weight, first, second)


def normalize(values):
    center = values - jnp.mean(values, axis=-1, keepdims=True)
    spread = jnp.mean(center * center, axis=-1, keepdims=True)
    scale = lax.rsqrt(spread + norm_eps)
    return center * scale, scale


def norm_back(grad, normed, scale):
    mean_g = jnp.mean(grad, axis=-1, keepdims=True)
    mean_gn = jnp.mean(grad * normed, axis=-1, keepdims=True)
    return (grad - mean_g - normed * mean_gn) * scale


def matmul(left, right):
    return jnp.dot(left, right, preferred_element_type=f32)


def column_sums(values):
    return jnp.sum(values.astype(f32), axis=0)


def tree_sum(parts):
    while len(parts) > 1:
        parts = [parts[i] + parts[i + 1] for i in range(0, len(parts), 2)]
    return parts[0]


def xor_take(values, mask):
    order = jnp.arange(values.shape[0], dtype=jnp.int32) ^ mask
    return jnp.take(values, order, axis=0, mode="clip")


def xor_parts(parts, mask):
    step = 1
    while step < len(parts):
        turned = (mask & step) != 0
        parts = [jnp.where(turned, parts[i ^ step], parts[i]) for i in range(len(parts))]
        step *= 2
    return parts


def attention_back(qkv_ref, d_att_ref, out_ref, d_keys, d_values):
    at = pl.program_id(1)
    hd = d_att_ref.shape[2]
    first = pl.multiple_of(at * QUERIES, QUERIES)

    @pl.when(at == 0)
    def _():
        d_keys[...] = jnp.zeros_like(d_keys)
        d_values[...] = jnp.zeros_like(d_values)

    def dot(left, right, dims):
        return lax.dot_general(left, right, (dims, ((), ())), preferred_element_type=f32)

    d_queries, k_parts, v_parts = [], [], []
    for head in range(hd // HEAD):
        low = head * HEAD
        query = qkv_ref[0, pl.ds(first, QUERIES), low : low + HEAD]
        key = qkv_ref[0, :, hd + low : hd + low + HEAD]
        value = qkv_ref[0, :, 2 * hd + low : 2 * hd + low + HEAD]
        d_att = d_att_ref[0, :, low : low + HEAD]
        scores = dot(query, key, ((1,), (1,))) * HEAD ** (-0.5)
        probs = jnp.exp(scores - jnp.max(scores, axis=1, keepdims=True))
        probs = probs / jnp.sum(probs, axis=1, keepdims=True)
        v_parts.append(dot(probs.astype(bf16), d_att, ((0,), (0,))))
        d_probs = dot(d_att, value, ((1,), (1,)))
        row_term = jnp.sum(probs * d_probs, axis=1, keepdims=True)
        d_scores = (probs * (d_probs - row_term)).astype(bf16)
        d_queries.append(dot(d_scores, key, ((1,), (0,))) * HEAD ** (-0.5))
        k_parts.append(dot(d_scores, query, ((0,), (0,))) * HEAD ** (-0.5))
    d_keys[...] += jnp.concatenate(k_parts, axis=1)
    d_values[...] += jnp.concatenate(v_parts, axis=1)
    out_ref[0, pl.ds(first, QUERIES), :hd] = jnp.concatenate(d_queries, axis=1).astype(bf16)

    @pl.when(at == pl.num_programs(1) - 1)
    def _():
        out_ref[0, :, hd : 2 * hd] = d_keys[...].astype(bf16)
        out_ref[0, :, 2 * hd :] = d_values[...].astype(bf16)


def attention_grads(qkv, d_att):
    images, _, hd = d_att.shape
    return pl.pallas_call(
        attention_back,
        grid=(images, SEQ_LEN // QUERIES),
        in_specs=[
            pl.BlockSpec((1, SEQ_LEN, 3 * hd), lambda i, j: (i, 0, 0)),
            pl.BlockSpec((1, QUERIES, hd), lambda i, j: (i, j, 0)),
        ],
        out_specs=pl.BlockSpec((1, SEQ_LEN, 3 * hd), lambda i, j: (i, 0, 0)),
        out_shape=jax.ShapeDtypeStruct((images, SEQ_LEN, 3 * hd), bf16),
        scratch_shapes=[pltpu.VMEM((SEQ_LEN, hd), f32), pltpu.VMEM((SEQ_LEN, hd), f32)],
        compiler_params=pltpu.CompilerParams(vmem_limit_bytes=40 * 1024 * 1024),
        cost_estimate=pl.CostEstimate(
            flops=10 * images * SEQ_LEN * SEQ_LEN * hd,
            bytes_accessed=14 * images * SEQ_LEN * hd,
            transcendentals=images * SEQ_LEN * SEQ_LEN * hd // HEAD,
        ),
    )(qkv, d_att)


def make_shards(n_f, n_z):
    n_s = n_z * CORES
    n_g = n_f * n_s
    heads_dev = HEADS // n_s
    hd = heads_dev * HEAD
    ub = FF // n_g
    rows = D // n_g
    units = n_z * ub

    def swap(values, axis, size, k):
        if k == 0:
            return values
        return lax.ppermute(values, axis, [(i, i ^ k) for i in range(size)])

    def swap_f(values, k):
        return swap(values, "fsdp", n_f, k)

    def swap_z(values, k):
        return swap(values, "z", n_z, k)

    def swap_c(values):
        return swap(values, "core", CORES, 1)

    def all_z(values):
        return [swap_z(values, k) for k in range(n_z)]

    def all_f(values):
        return [swap_f(values, k) for k in range(n_f)]


    def run(*chains):
        results = [None] * len(chains)
        pending = {}
        for i, chain in enumerate(chains):
            try:
                pending[i] = next(chain)
            except StopIteration as stop:
                results[i] = stop.value
        while pending:
            leaves, tree = jax.tree.flatten(pending)
            if len(leaves) > 1:
                leaves = lax.optimization_barrier(leaves)
            came = jax.tree.unflatten(tree, leaves)
            pending = {}
            for i, value in came.items():
                try:
                    pending[i] = chains[i].send(value)
                except StopIteration as stop:
                    results[i] = stop.value
        return results

    def alone(chain):
        return run(chain)[0]

    def double(values, swap_with, size):
        values = values[None]
        step = 1
        while step < size:
            came = yield swap_with(values, step)
            values = jnp.concatenate([values, came])
            step *= 2
        return values

    def shift(entries, swap_with):
        entries = list(entries)
        step = 1
        while step < len(entries):
            moved = [k for k in range(len(entries)) if k & step]
            came = yield swap_with(jnp.stack([entries[k] for k in moved]), step)
            for i, k in enumerate(moved):
                entries[k] = came[i]
            step *= 2
        return entries

    def halve(parts, swap_with, kind=bf16):
        parts = list(parts)
        step = len(parts) // 2
        while step > 0:
            low = jnp.stack([parts[k + step] for k in range(step)]).astype(kind)
            came = yield swap_with(low, step)
            parts = [parts[k] + came[k].astype(f32) for k in range(step)]
            step //= 2
        return parts[0]

    def halve_near(parts, swap_with):
        parts = list(parts)
        step = 1
        while len(parts) > 1:
            low = jnp.stack(parts[1::2]).astype(bf16)
            came = yield swap_with(low, step)
            parts = [part + came[i].astype(f32) for i, part in enumerate(parts[0::2])]
            step *= 2
        return parts[0]

    def resume(chain, came, done=None):
        if came is None:
            return done
        try:
            came = chain.send(came)
        except StopIteration as stop:
            return stop.value
        while True:
            came = yield came
            try:
                came = chain.send(came)
            except StopIteration as stop:
                return stop.value

    def add_z(values):
        step = 1
        while step < n_z:
            came = yield swap_z(values, step)
            values = values + came
            step *= 2
        return values

    def add_seq(values):
        came = yield swap_c(values)
        values = yield from add_z(values + came)
        return values

    def after(value, *others):
        return lax.optimization_barrier((value,) + others)[0]

    def join_cores(values):
        low = values[:, 1].astype(bf16)
        return [
            values[k, 0] + swap_c(low[k]).astype(f32) for k in range(values.shape[0])
        ]

    def with_cores(pieces):
        return jnp.concatenate([part for own in pieces for part in (own, swap_c(own))])

    def add_parts(own, parts):
        return tree_sum([own] + [part.astype(f32) for part in parts])

    def shards(
        tokens,
        condition,
        block_image,
        cotangent,
        modul_weight,
        qkv_weight,
        proj_weight,
        widen_weight,
        narrow_weight,
        bias_vector,
        modul_mean,
        qkv_mean,
        proj_mean,
        widen_mean,
        narrow_mean,
        bias_mean,
        modul_square,
        qkv_square,
        proj_square,
        widen_square,
        narrow_square,
        bias_square,
    ):
        images_group = condition.shape[0]
        tok_group = n_s * BLOCK
        head_scale = HEAD ** (-0.5)
        at_f = lax.axis_index("fsdp")
        at_z = lax.axis_index("z")
        at_c = lax.axis_index("core")
        at_s = at_z * CORES + at_c
        at_g = at_f * n_s + at_s
        first_core = at_c == 0
        local_ids = block_image - at_f * images_group

        pick_f = (jnp.arange(n_f) == at_f).astype(f32)
        pick_c = (jnp.arange(CORES) == at_c).astype(f32)
        pick_s = (jnp.arange(n_s) == at_s).astype(f32)

        def by_core(zero, one):
            return jnp.where(first_core, zero, one), jnp.where(first_core, one, zero)

        def trade_cores(zeros, ones):
            pairs = [by_core(zero, one) for zero, one in zip(zeros, ones)]
            came = yield swap_c(jnp.stack([other for _, other in pairs]))
            return [by_core(own, came[i]) for i, (own, _) in enumerate(pairs)]

        def trade_seq(entries):
            pairs = yield from trade_cores(entries[0::2], entries[1::2])
            pairs = xor_parts([jnp.stack(pair) for pair in pairs], at_z)
            pairs = xor_parts((yield from shift(pairs, swap_z)), at_z)
            return [pairs[i // 2][i % 2] for i in range(n_s)]

        def trade_mlp(entries):
            pairs = yield from trade_cores(entries[0::2], entries[1::2])
            pairs = xor_parts([jnp.stack(pair) for pair in pairs], at_f)
            pairs = xor_parts((yield from shift(pairs, swap_f)), at_f)
            return [pairs[i // 2][i % 2] for i in range(n_f * CORES)]

        width = bias_vector.shape[0]
        modul_low = modul_weight.astype(bf16)
        tokens_z = all_z(tokens)
        tokens_group = with_cores(tokens_z).reshape(n_s, BLOCK, D)

        qkv_low = qkv_weight.astype(bf16).reshape(rows, 3, n_s, hd)

        proj_full = lax.all_gather(
            proj_weight.astype(bf16), ("fsdp", "z", "core"), axis=0, tiled=True
        )

        cond_float = condition.astype(f32)

        def modul_chain():
            small = yield from double(
                jnp.concatenate([condition.reshape(-1), bias_vector.astype(bf16)]), swap_f, n_f
            )
            cond_all = small[:, : images_group * D].reshape(n_f * images_group, D).astype(f32)
            all_act = jax.nn.silu(cond_all).astype(bf16)
            act_cols = lax.dynamic_slice_in_dim(all_act, at_g * rows, rows, axis=1)
            part = matmul(act_cols, modul_low).reshape(n_f, images_group, 6 * D)
            due = [part[k] for k in range(n_f)]
            while len(due) > 1:
                half = len(due) // 2
                low = jnp.stack(due[half:])
                if half == 1:
                    low = after(low, *tokens_z[1:])
                came = yield swap_f(low, half)
                due = [due[k] + came[k] for k in range(half)]
            part = due[0]
            bias_rows = xor_parts([small[k, images_group * D :] for k in range(n_f)], at_f)
            bias_rows = jnp.stack(bias_rows).astype(f32)
            placed = (bias_rows[:, None, :] * pick_s[None, :, None]).reshape(-1)
            part = (part + placed[: 6 * D]).reshape(-1)
            return act_cols, jnp.concatenate([part, placed[6 * D :]])

        widen_low = widen_weight.astype(bf16).reshape(rows, n_f, n_z, CORES, ub)
        (act_cols, whole), qkv_mine, widen_mine = run(
            modul_chain(),
            trade_seq([qkv_low[:, :, i].reshape(rows, 3 * hd) for i in range(n_s)]),
            trade_mlp(
                [
                    widen_low[:, i // CORES, :, i % CORES].reshape(rows, units)
                    for i in range(n_f * CORES)
                ]
            ),
        )
        qkv_parts = all_f(jnp.stack(qkv_mine))
        qkv_full = jnp.stack(xor_parts(qkv_parts, at_f)).reshape(D, 3 * hd)
        whole = whole + swap_c(whole)
        near = 1
        while near < n_z:
            if 2 * near == n_z:
                whole = after(whole, *qkv_parts[1:])
            whole = whole + swap_z(whole, near)
            near *= 2
        modulation = whole[: images_group * 6 * D].reshape(images_group, 6 * D)
        bias_all = whole[images_group * 6 * D :]
        bias_query = bias_all[:D].reshape(n_s, hd)
        bias_value = bias_all[D : 2 * D].reshape(n_s, hd)
        bias_proj = bias_all[2 * D : 3 * D]
        bias_widen = bias_all[3 * D : 3 * D + FF].reshape(n_f, n_z, CORES, ub)
        bias_narrow = bias_all[3 * D + FF :]

        widen_full = lax.all_gather(jnp.concatenate(widen_mine), "z", axis=0, tiled=False)
        widen_full = widen_full.reshape(n_z, n_f, CORES * rows, units)
        widen_full = widen_full.transpose(1, 0, 2, 3).reshape(D, units)
        narrow_late = after(narrow_weight, *widen_mine).astype(bf16)
        narrow_full = lax.all_gather(narrow_late, "z", axis=0, tiled=True)

        own_id = lax.dynamic_index_in_dim(local_ids, at_s, keepdims=False)
        image_pick = (own_id == jnp.arange(images_group, dtype=jnp.int32)).astype(f32)
        if images_group == 1:
            own_row = modulation[0]
            group_rows = modulation
        else:
            own_row = jnp.sum(image_pick[:, None] * modulation, axis=0)
            rel_ids = xor_take(local_ids, at_s)
            rel_pick = (
                rel_ids[:, None] == jnp.arange(images_group, dtype=jnp.int32)[None, :]
            ).astype(f32)
            group_rows = jnp.sum(rel_pick[:, :, None] * modulation[None, :, :], axis=1)
            arrange = jnp.argsort(rel_ids, stable=True)
            restore = jnp.argsort(arrange, stable=True)
        shift_a, scale_a, gate_a, shift_b, scale_b, gate_b = [
            own_row[i * D : (i + 1) * D] for i in range(6)
        ]

        def by_image(values):
            if images_group > 1:
                values = values.reshape(n_s, BLOCK, hd)[arrange]
            values = values.reshape(images_group, SEQ_LEN, heads_dev, HEAD)
            return values.transpose(0, 2, 1, 3)

        def by_block(values):
            values = values.transpose(0, 2, 1, 3).reshape(tok_group, hd)
            if images_group > 1:
                values = values.reshape(n_s, BLOCK, hd)[restore].reshape(tok_group, hd)
            return values

        def send_blocks(values):
            came = swap_c(values[:, 1])
            parts = [swap_z(jnp.stack([values[k, 0], came[k]]), k) for k in range(n_z)]
            pairs = [by_core(part[0], part[1]) for part in xor_parts(parts, at_z)]
            return jnp.concatenate([part for pair in pairs for part in pair], axis=1)

        def send_heads(values):
            parts = [values[:, i * hd : (i + 1) * hd] for i in range(n_s)]
            pairs = [by_core(parts[2 * i], parts[2 * i + 1]) for i in range(n_z)]
            own = xor_parts([pair[0] for pair in pairs], at_z)
            other = xor_parts([pair[1] for pair in pairs], at_z)
            came = swap_c(jnp.stack(other))
            parts = [swap_z(jnp.stack([own[k], came[k]]), k) for k in range(n_z)]
            return jnp.stack(parts).reshape(tok_group, hd)

        grad_out = cotangent.astype(f32)
        d_b_own = (gate_b * grad_out).astype(bf16)

        normed_group, _ = normalize(tokens_group.astype(f32))
        h_a = (
            normed_group * (1.0 + group_rows[:, None, D : 2 * D]) + group_rows[:, None, :D]
        ).astype(bf16)
        h_a = h_a.reshape(tok_group, D)
        query_bias = lax.dynamic_index_in_dim(bias_query, at_s, keepdims=False)
        value_bias = lax.dynamic_index_in_dim(bias_value, at_s, keepdims=False)
        qkv_bias = jnp.concatenate([query_bias, jnp.zeros((hd,), f32), value_bias])
        qkv = (matmul(h_a, qkv_full) + qkv_bias).astype(bf16)
        queries = by_image(qkv[:, :hd])
        keys = by_image(qkv[:, hd : 2 * hd])
        values = by_image(qkv[:, 2 * hd :])
        scores = (
            jnp.einsum("ihqd,ihkd->ihqk", queries, keys, preferred_element_type=f32) * head_scale
        )
        log_total = jax.nn.logsumexp(scores, axis=-1, keepdims=True)
        probs = jnp.exp(scores - log_total)
        probs_low = probs.astype(bf16)
        attended = by_block(
            jnp.einsum("ihqk,ihkd->ihqd", probs_low, values, preferred_element_type=f32).astype(
                bf16
            )
        )
        attended = after(attended, proj_full)
        att_own = send_blocks(attended.reshape(n_z, CORES, BLOCK, hd))

        branch_a = matmul(att_own, proj_full) + bias_proj
        inputs = tokens.astype(f32)
        middle = inputs + gate_a * branch_a
        normed_b, spread_b = normalize(middle)
        h_b_own = (normed_b * (1.0 + scale_b) + shift_b).astype(bf16)

        d_b_f = after(alone(double(d_b_own, swap_f, n_f)), h_b_own)
        modul_rows = lax.all_gather(after(modul_low, h_b_own), "fsdp", axis=0, tiled=True)
        d_b = with_cores([d_b_f[k] for k in range(n_f)])
        h_b = with_cores(all_f(h_b_own))
        bias_units = lax.dynamic_index_in_dim(bias_widen, at_f, 0, keepdims=False)
        bias_units = lax.dynamic_index_in_dim(bias_units, at_c, 1, keepdims=False).reshape(units)
        widened = matmul(h_b, widen_full) + bias_units
        activated, gelu_pull = jax.vjp(lambda u: jax.nn.gelu(u, approximate=True), widened)
        activated = activated.astype(bf16)
        d_act = jnp.einsum("td,fd->tf", d_b, narrow_full, preferred_element_type=f32)
        d_wide = gelu_pull(d_act)[0].astype(bf16)
        d_hb_part = jnp.einsum("tf,df->td", d_wide, widen_full, preferred_element_type=f32)
        d_hb_f = join_cores(d_hb_part.reshape(n_f, CORES, BLOCK, D))
        d_hb_came = [swap_f(d_hb_f[k].astype(bf16), k) for k in range(1, n_f)]
        grad_narrow = jnp.einsum("tf,td->fd", activated, d_b, preferred_element_type=f32)
        grad_narrow = after(grad_narrow, *d_hb_f).reshape(n_z, ub, D)
        narrow_chain = halve_near(
            [
                lax.dynamic_index_in_dim(grad_narrow, at_z ^ k, 0, keepdims=False)
                for k in range(n_z)
            ],
            swap_z,
        )
        narrow_came = next(narrow_chain)
        d_hb = add_parts(d_hb_f[0], [after(part, narrow_came) for part in d_hb_came])
        branch_part = matmul(activated, narrow_full).reshape(n_f, CORES, BLOCK, D)
        grad_widen = jnp.einsum("td,tf->df", h_b, d_wide, preferred_element_type=f32)
        grad_widen = grad_widen.astype(bf16).reshape(n_f, n_z, CORES, rows, units)
        grad_widen = grad_widen.transpose(1, 0, 2, 3, 4).reshape(n_z, -1, units)

        d_shift_b = jnp.sum(d_hb, axis=0)
        d_scale_b = jnp.sum(d_hb * normed_b, axis=0)
        d_middle = grad_out + norm_back(d_hb * (1.0 + scale_b), normed_b, spread_b)
        d_gate_a = jnp.sum(d_middle * branch_a, axis=0)
        d_a = (gate_a * d_middle).astype(bf16)
        d_att_own = jnp.einsum("te,de->td", d_a, proj_full, preferred_element_type=f32)
        d_att_own = d_att_own.astype(bf16)
        d_att = send_heads(d_att_own)
        grad_proj = jnp.einsum(
            "td,te->de", att_own, after(d_a, d_att_own), preferred_element_type=f32
        )
        grad_proj = grad_proj.reshape(n_f, n_z, CORES, rows, D)
        proj_own, proj_other = by_core(grad_proj[:, :, 0], grad_proj[:, :, 1])

        branch_chain = halve(join_cores(after(branch_part, d_hb)), swap_f)
        branch_came = next(branch_chain)

        def further(chain, came):
            try:
                return chain.send(came), None
            except StopIteration as stop:
                return None, stop.value

        narrow_came, narrow_sum = further(narrow_chain, narrow_came)
        if narrow_came is not None:
            d_att, narrow_came, branch_came = lax.optimization_barrier(
                (d_att, narrow_came, branch_came)
            )
        else:
            d_att, branch_came = lax.optimization_barrier((d_att, branch_came))
        branch_came, branch_b = further(branch_chain, branch_came)
        grad_widen = after(grad_widen, d_att)
        widen_part = lax.psum_scatter(grad_widen, "z", scatter_dimension=0, tiled=False)
        def in_images(values, order):
            if images_group > 1:
                values = values.reshape(n_s, BLOCK, -1)[order]
            return values.reshape(images_group, SEQ_LEN, -1)

        proj_both = proj_own + swap_c(proj_other.astype(bf16)).astype(f32)

        order = None if images_group == 1 else arrange
        d_qkv = attention_grads(in_images(qkv, order), in_images(d_att, order))
        if images_group > 1:
            d_qkv = d_qkv.reshape(n_s, BLOCK, 3 * hd)[restore]
        d_qkv = d_qkv.reshape(tok_group, 3 * hd)
        if branch_came is not None:
            d_qkv, branch_came, proj_both = lax.optimization_barrier(
                (d_qkv, branch_came, proj_both)
            )
        else:
            d_qkv, proj_both = lax.optimization_barrier((d_qkv, proj_both))
        proj_chain = halve(
            [
                lax.dynamic_index_in_dim(proj_both, at_f ^ k, 0, keepdims=False)
                for k in range(n_f)
            ],
            swap_f,
        )
        d_ha_part = jnp.einsum("te,de->td", d_qkv, qkv_full, preferred_element_type=f32)
        d_ha_z = join_cores(d_ha_part.reshape(n_z, CORES, BLOCK, D))
        d_ha_low = [d_ha_z[k].astype(bf16) for k in range(1, n_z)]
        d_ha_came = [swap_z(d_ha_low[k - 1], k) for k in range(1, n_z)]
        grad_qkv = jnp.einsum("td,te->de", h_a, d_qkv, preferred_element_type=f32)
        grad_qkv = after(grad_qkv.reshape(n_f, n_s * rows, 3 * hd), *d_ha_low)
        grad_qkv = [
            lax.dynamic_index_in_dim(grad_qkv, at_f ^ k, 0, keepdims=False) for k in range(n_f)
        ]
        widen_part = after(widen_part, *d_ha_low).reshape(n_f * CORES, rows, units)

        if branch_came is not None:
            branch_b = alone(resume(branch_chain, branch_came))
        if narrow_came is not None:
            narrow_sum = alone(resume(narrow_chain, narrow_came))
        proj_came = next(proj_chain)
        qkv_chain = halve(grad_qkv, swap_f)
        qkv_came = next(qkv_chain)
        widen_chain = trade_mlp([widen_part[i] for i in range(n_f * CORES)])
        widen_came = next(widen_chain)
        d_ha = add_parts(d_ha_z[0], d_ha_came)
        branch_b = branch_b + bias_narrow
        block_output = (middle + gate_b * branch_b).astype(bf16)
        d_gate_b = jnp.sum(grad_out * branch_b, axis=0)
        normed_a, spread_a = normalize(inputs)
        d_shift_a = jnp.sum(d_ha, axis=0)
        d_scale_a = jnp.sum(d_ha * normed_a, axis=0)
        tokens_grad = (
            d_middle + norm_back(d_ha * (1.0 + scale_a), normed_a, spread_a)
        ).astype(bf16)

        units_sum = column_sums(d_wide).reshape(n_z, ub)
        bias_g_widen = (
            pick_f[:, None, None, None] * pick_c[None, None, :, None] * units_sum[None, :, None, :]
        ).reshape(FF)
        heads_sum = column_sums(d_qkv)
        bias_g_query = (pick_s[:, None] * heads_sum[None, :hd]).reshape(D)
        bias_g_value = (pick_s[:, None] * heads_sum[None, 2 * hd :]).reshape(D)
        d_block = jnp.concatenate([d_shift_a, d_scale_a, d_gate_a, d_shift_b, d_scale_b, d_gate_b])
        per_image = (image_pick[:, None] * d_block[None, :]).reshape(-1)
        pieces = [
            per_image,
            bias_g_query,
            bias_g_value,
            column_sums(d_a),
            bias_g_widen,
            column_sums(d_b_own),
        ]
        sums, proj_mid, qkv_mid, widen_back = run(
            add_seq(jnp.concatenate(pieces)),
            resume(proj_chain, proj_came),
            resume(qkv_chain, qkv_came),
            resume(widen_chain, widen_came),
        )
        widen_sum = jnp.stack(widen_back).reshape(n_f, CORES, rows, n_z, ub)
        widen_sum = widen_sum.transpose(2, 0, 3, 1, 4).reshape(rows, FF).astype(f32)
        cut = images_group * 6 * D
        d_own = sums[:cut].reshape(images_group, 6 * D)
        d_cond_rows = jnp.einsum(
            "im,dm->id",
            d_own,
            modul_rows.astype(f32),
            precision=lax.Precision.HIGHEST,
            preferred_element_type=f32,
        )

        def cond_chain():
            part = yield from double(d_cond_rows, swap_z, n_z)
            part = jnp.stack(xor_parts([part[k] for k in range(n_z)], at_z))
            came = yield swap_c(part)
            return jnp.stack(by_core(part, came), axis=1)

        whole, d_cond, proj_sum, qkv_sum = run(
            double(sums, swap_f, n_f),
            cond_chain(),
            halve(xor_parts([proj_mid[k] for k in range(n_z)], at_z), swap_z),
            trade_seq([qkv_mid[i : i + rows] for i in range(0, n_s * rows, rows)]),
        )
        qkv_sum = jnp.stack(qkv_sum).reshape(n_s, rows, 3, hd)
        qkv_sum = qkv_sum.transpose(1, 2, 0, 3).reshape(rows, 3 * D)
        d_cond = d_cond.reshape(n_s, images_group, n_f, rows)
        d_cond_act = d_cond.transpose(1, 2, 0, 3).reshape(images_group, D)
        silu_pull = jax.vjp(jax.nn.silu, cond_float)[1]
        condition_grad = silu_pull(d_cond_act)[0]

        d_modulation = whole[:, :cut].reshape(n_f * images_group, 6 * D)
        act_wide = act_cols.astype(f32)
        modul_sum = sum(
            act_wide[i][:, None] * d_modulation[i][None, :] for i in range(n_f * images_group)
        )
        bias_grad = jnp.concatenate(
            [jnp.sum(d_modulation, axis=0), jnp.sum(whole[:, cut:], axis=0)]
        )
        bias_sum = lax.dynamic_slice_in_dim(bias_grad, at_g * width, width)

        rate_wide = 2.0 / math.sqrt(D)
        modul_new = adam_step(modul_weight, modul_sum, modul_mean, modul_square, rate_wide)
        qkv_new = adam_step(qkv_weight, qkv_sum, qkv_mean, qkv_square, rate_wide)
        proj_new = adam_step(
            proj_weight, proj_sum, proj_mean, proj_square, 2.0 / math.sqrt(D // 16)
        )
        widen_new = adam_step(widen_weight, widen_sum, widen_mean, widen_square, rate_wide)
        narrow_new = adam_step(
            narrow_weight, narrow_sum, narrow_mean, narrow_square, 2.0 / math.sqrt(FF)
        )
        bias_new = adam_step(bias_vector, bias_sum, bias_mean, bias_square, 0.5)
        news = (modul_new, qkv_new, proj_new, widen_new, narrow_new, bias_new)
        return (
            block_output,
            tokens_grad,
            condition_grad,
            *[new[0] for new in news],
            *[new[1] for new in news],
            *[new[2] for new in news],
        )

    return shards


def solution(mesh):
    n_f, n_s = mesh.shape["fsdp"], mesh.shape["seq"]
    n_z = n_s // CORES
    cores = jax.sharding.Mesh(mesh.devices.reshape(n_f, n_z, CORES), ("fsdp", "z", "core"))
    both = P(("fsdp", "z", "core"), None)
    flat = P(("fsdp", "z", "core"))
    params = (both, both, both, both, both, flat)
    return jax.shard_map(
        make_shards(n_f, n_z),
        mesh=cores,
        in_specs=(both, P("fsdp", None), P("fsdp"), both) + params * 3,
        out_specs=(both, both, P("fsdp", None)) + params * 3,
        check_vma=False,
    )
```

```python
import math

import jax
import jax.numpy as jnp
from jax import lax
from jax.experimental import pallas as pl
from jax.experimental.pallas import tpu as pltpu
from jax.sharding import PartitionSpec as P

D = 1024
HEADS = 16
HEAD = 64
FF = 4096
BLOCK = 128
SEQ_LEN = 1024
STEP = 10

CORES = 2
QUERIES = 256

norm_eps = 1e-06
beta_first = 0.9
beta_second = 0.95
adam_eps = 1e-08
decay_rate = 0.01

f32 = jnp.float32
bf16 = jnp.bfloat16


def adam_step(weight, grad, first, second, rate):
    first = beta_first * first + (1.0 - beta_first) * grad
    second = beta_second * second + (1.0 - beta_second) * grad * grad
    fix_first = 1.0 - beta_first**STEP
    fix_second = 1.0 - beta_second**STEP
    weight = weight - rate * (
        first / fix_first / (jnp.sqrt(second / fix_second) + adam_eps) + decay_rate * weight
    )
    return (weight, first, second)


def normalize(values):
    center = values - jnp.mean(values, axis=-1, keepdims=True)
    spread = jnp.mean(center * center, axis=-1, keepdims=True)
    scale = lax.rsqrt(spread + norm_eps)
    return center * scale, scale


def norm_back(grad, normed, scale):
    mean_g = jnp.mean(grad, axis=-1, keepdims=True)
    mean_gn = jnp.mean(grad * normed, axis=-1, keepdims=True)
    return (grad - mean_g - normed * mean_gn) * scale


def matmul(left, right):
    return jnp.dot(left, right, preferred_element_type=f32)


def column_sums(values):
    return jnp.sum(values.astype(f32), axis=0)


def tree_sum(parts):
    while len(parts) > 1:
        parts = [parts[i] + parts[i + 1] for i in range(0, len(parts), 2)]
    return parts[0]


def xor_take(values, mask):
    order = jnp.arange(values.shape[0], dtype=jnp.int32) ^ mask
    return jnp.take(values, order, axis=0, mode="clip")


def xor_parts(parts, mask):
    step = 1
    while step < len(parts):
        turned = (mask & step) != 0
        parts = [jnp.where(turned, parts[i ^ step], parts[i]) for i in range(len(parts))]
        step *= 2
    return parts


def attention_back(qkv_ref, d_att_ref, out_ref, d_keys, d_values):
    at = pl.program_id(1)
    hd = d_att_ref.shape[2]
    first = pl.multiple_of(at * QUERIES, QUERIES)

    @pl.when(at == 0)
    def _():
        d_keys[...] = jnp.zeros_like(d_keys)
        d_values[...] = jnp.zeros_like(d_values)

    def dot(left, right, dims):
        return lax.dot_general(left, right, (dims, ((), ())), preferred_element_type=f32)

    d_queries, k_parts, v_parts = [], [], []
    for head in range(hd // HEAD):
        low = head * HEAD
        query = qkv_ref[0, pl.ds(first, QUERIES), low : low + HEAD]
        key = qkv_ref[0, :, hd + low : hd + low + HEAD]
        value = qkv_ref[0, :, 2 * hd + low : 2 * hd + low + HEAD]
        d_att = d_att_ref[0, :, low : low + HEAD]
        scores = dot(query, key, ((1,), (1,))) * HEAD ** (-0.5)
        probs = jnp.exp(scores - jnp.max(scores, axis=1, keepdims=True))
        probs = probs / jnp.sum(probs, axis=1, keepdims=True)
        v_parts.append(dot(probs.astype(bf16), d_att, ((0,), (0,))))
        d_probs = dot(d_att, value, ((1,), (1,)))
        row_term = jnp.sum(probs * d_probs, axis=1, keepdims=True)
        d_scores = (probs * (d_probs - row_term)).astype(bf16)
        d_queries.append(dot(d_scores, key, ((1,), (0,))) * HEAD ** (-0.5))
        k_parts.append(dot(d_scores, query, ((0,), (0,))) * HEAD ** (-0.5))
    d_keys[...] += jnp.concatenate(k_parts, axis=1)
    d_values[...] += jnp.concatenate(v_parts, axis=1)
    out_ref[0, pl.ds(first, QUERIES), :hd] = jnp.concatenate(d_queries, axis=1).astype(bf16)

    @pl.when(at == pl.num_programs(1) - 1)
    def _():
        out_ref[0, :, hd : 2 * hd] = d_keys[...].astype(bf16)
        out_ref[0, :, 2 * hd :] = d_values[...].astype(bf16)


def attention_forward(qkv_ref, out_ref):
    hd = out_ref.shape[2]
    first = pl.multiple_of(pl.program_id(1) * QUERIES, QUERIES)
    parts = []
    for head in range(hd // HEAD):
        low = head * HEAD
        query = qkv_ref[0, pl.ds(first, QUERIES), low : low + HEAD]
        key = qkv_ref[0, :, hd + low : hd + low + HEAD]
        value = qkv_ref[0, :, 2 * hd + low : 2 * hd + low + HEAD]
        scores = lax.dot_general(
            query, key, (((1,), (1,)), ((), ())), preferred_element_type=f32
        ) * HEAD ** (-0.5)
        probs = jnp.exp(scores - jnp.max(scores, axis=1, keepdims=True))
        probs = (probs / jnp.sum(probs, axis=1, keepdims=True)).astype(bf16)
        parts.append(jnp.dot(probs, value, preferred_element_type=f32))
    out_ref[0] = jnp.concatenate(parts, axis=1).astype(bf16)


def attention(qkv):
    images, _, wide = qkv.shape
    hd = wide // 3
    return pl.pallas_call(
        attention_forward,
        grid=(images, SEQ_LEN // QUERIES),
        in_specs=[pl.BlockSpec((1, SEQ_LEN, wide), lambda i, j: (i, 0, 0))],
        out_specs=pl.BlockSpec((1, QUERIES, hd), lambda i, j: (i, j, 0)),
        out_shape=jax.ShapeDtypeStruct((images, SEQ_LEN, hd), bf16),
        compiler_params=pltpu.CompilerParams(vmem_limit_bytes=40 * 1024 * 1024),
        cost_estimate=pl.CostEstimate(
            flops=4 * images * SEQ_LEN * SEQ_LEN * hd,
            bytes_accessed=8 * images * SEQ_LEN * hd,
            transcendentals=images * SEQ_LEN * SEQ_LEN * hd // HEAD,
        ),
    )(qkv)


def attention_grads(qkv, d_att):
    images, _, hd = d_att.shape
    return pl.pallas_call(
        attention_back,
        grid=(images, SEQ_LEN // QUERIES),
        in_specs=[
            pl.BlockSpec((1, SEQ_LEN, 3 * hd), lambda i, j: (i, 0, 0)),
            pl.BlockSpec((1, QUERIES, hd), lambda i, j: (i, j, 0)),
        ],
        out_specs=pl.BlockSpec((1, SEQ_LEN, 3 * hd), lambda i, j: (i, 0, 0)),
        out_shape=jax.ShapeDtypeStruct((images, SEQ_LEN, 3 * hd), bf16),
        scratch_shapes=[pltpu.VMEM((SEQ_LEN, hd), f32), pltpu.VMEM((SEQ_LEN, hd), f32)],
        compiler_params=pltpu.CompilerParams(vmem_limit_bytes=40 * 1024 * 1024),
        cost_estimate=pl.CostEstimate(
            flops=10 * images * SEQ_LEN * SEQ_LEN * hd,
            bytes_accessed=14 * images * SEQ_LEN * hd,
            transcendentals=images * SEQ_LEN * SEQ_LEN * hd // HEAD,
        ),
    )(qkv, d_att)


def make_shards(n_f, n_z):
    n_s = n_z * CORES
    n_g = n_f * n_s
    heads_dev = HEADS // n_s
    hd = heads_dev * HEAD
    ub = FF // n_g
    rows = D // n_g
    units = n_z * ub

    def swap(values, axis, size, k):
        if k == 0:
            return values
        return lax.ppermute(values, axis, [(i, i ^ k) for i in range(size)])

    def swap_f(values, k):
        return swap(values, "fsdp", n_f, k)

    def swap_z(values, k):
        return swap(values, "z", n_z, k)

    def swap_c(values):
        return swap(values, "core", CORES, 1)

    def all_z(values):
        return [swap_z(values, k) for k in range(n_z)]

    def all_f(values):
        return [swap_f(values, k) for k in range(n_f)]


    def run(*chains):
        results = [None] * len(chains)
        pending = {}
        for i, chain in enumerate(chains):
            try:
                pending[i] = next(chain)
            except StopIteration as stop:
                results[i] = stop.value
        while pending:
            leaves, tree = jax.tree.flatten(pending)
            if len(leaves) > 1:
                leaves = lax.optimization_barrier(leaves)
            came = jax.tree.unflatten(tree, leaves)
            pending = {}
            for i, value in came.items():
                try:
                    pending[i] = chains[i].send(value)
                except StopIteration as stop:
                    results[i] = stop.value
        return results

    def alone(chain):
        return run(chain)[0]

    def double(values, swap_with, size):
        values = values[None]
        step = 1
        while step < size:
            came = yield swap_with(values, step)
            values = jnp.concatenate([values, came])
            step *= 2
        return values

    def shift(entries, swap_with):
        entries = list(entries)
        step = 1
        while step < len(entries):
            moved = [k for k in range(len(entries)) if k & step]
            came = yield swap_with(jnp.stack([entries[k] for k in moved]), step)
            for i, k in enumerate(moved):
                entries[k] = came[i]
            step *= 2
        return entries

    def halve(parts, swap_with, kind=bf16):
        parts = list(parts)
        step = len(parts) // 2
        while step > 0:
            low = jnp.stack([parts[k + step] for k in range(step)]).astype(kind)
            came = yield swap_with(low, step)
            parts = [parts[k] + came[k].astype(f32) for k in range(step)]
            step //= 2
        return parts[0]

    def halve_near(parts, swap_with):
        parts = list(parts)
        step = 1
        while len(parts) > 1:
            low = jnp.stack(parts[1::2]).astype(bf16)
            came = yield swap_with(low, step)
            parts = [part + came[i].astype(f32) for i, part in enumerate(parts[0::2])]
            step *= 2
        return parts[0]

    def resume(chain, came, done=None):
        if came is None:
            return done
        try:
            came = chain.send(came)
        except StopIteration as stop:
            return stop.value
        while True:
            came = yield came
            try:
                came = chain.send(came)
            except StopIteration as stop:
                return stop.value

    def add_z(values):
        step = 1
        while step < n_z:
            came = yield swap_z(values, step)
            values = values + came
            step *= 2
        return values

    def add_seq(values):
        came = yield swap_c(values)
        values = yield from add_z(values + came)
        return values

    def after(value, *others):
        return lax.optimization_barrier((value,) + others)[0]

    def join_cores(values):
        low = values[:, 1].astype(bf16)
        return [
            values[k, 0] + swap_c(low[k]).astype(f32) for k in range(values.shape[0])
        ]

    def with_cores(pieces):
        return jnp.concatenate([part for own in pieces for part in (own, swap_c(own))])

    def add_parts(own, parts):
        return tree_sum([own] + [part.astype(f32) for part in parts])

    def shards(
        tokens,
        condition,
        block_image,
        cotangent,
        modul_weight,
        qkv_weight,
        proj_weight,
        widen_weight,
        narrow_weight,
        bias_vector,
        modul_mean,
        qkv_mean,
        proj_mean,
        widen_mean,
        narrow_mean,
        bias_mean,
        modul_square,
        qkv_square,
        proj_square,
        widen_square,
        narrow_square,
        bias_square,
    ):
        images_group = condition.shape[0]
        tok_group = n_s * BLOCK
        head_scale = HEAD ** (-0.5)
        at_f = lax.axis_index("fsdp")
        at_z = lax.axis_index("z")
        at_c = lax.axis_index("core")
        at_s = at_z * CORES + at_c
        at_g = at_f * n_s + at_s
        first_core = at_c == 0
        local_ids = block_image - at_f * images_group

        pick_f = (jnp.arange(n_f) == at_f).astype(f32)
        pick_c = (jnp.arange(CORES) == at_c).astype(f32)
        pick_s = (jnp.arange(n_s) == at_s).astype(f32)

        def by_core(zero, one):
            return jnp.where(first_core, zero, one), jnp.where(first_core, one, zero)

        def trade_cores(zeros, ones):
            pairs = [by_core(zero, one) for zero, one in zip(zeros, ones)]
            came = yield swap_c(jnp.stack([other for _, other in pairs]))
            return [by_core(own, came[i]) for i, (own, _) in enumerate(pairs)]

        def trade_seq(entries):
            pairs = yield from trade_cores(entries[0::2], entries[1::2])
            pairs = xor_parts([jnp.stack(pair) for pair in pairs], at_z)
            pairs = xor_parts((yield from shift(pairs, swap_z)), at_z)
            return [pairs[i // 2][i % 2] for i in range(n_s)]

        def trade_mlp(entries):
            pairs = yield from trade_cores(entries[0::2], entries[1::2])
            pairs = xor_parts([jnp.stack(pair) for pair in pairs], at_f)
            pairs = xor_parts((yield from shift(pairs, swap_f)), at_f)
            return [pairs[i // 2][i % 2] for i in range(n_f * CORES)]

        width = bias_vector.shape[0]
        modul_low = modul_weight.astype(bf16)
        tokens_z = all_z(tokens)
        tokens_group = with_cores(tokens_z).reshape(n_s, BLOCK, D)

        qkv_low = qkv_weight.astype(bf16).reshape(rows, 3, n_s, hd)

        proj_full = lax.all_gather(
            proj_weight.astype(bf16), ("fsdp", "z", "core"), axis=0, tiled=True
        )

        cond_float = condition.astype(f32)

        def modul_chain():
            small = yield from double(
                jnp.concatenate([condition.reshape(-1), bias_vector.astype(bf16)]), swap_f, n_f
            )
            cond_all = small[:, : images_group * D].reshape(n_f * images_group, D).astype(f32)
            all_act = jax.nn.silu(cond_all).astype(bf16)
            act_cols = lax.dynamic_slice_in_dim(all_act, at_g * rows, rows, axis=1)
            part = matmul(act_cols, modul_low).reshape(n_f, images_group, 6 * D)
            due = [part[k] for k in range(n_f)]
            while len(due) > 1:
                half = len(due) // 2
                low = jnp.stack(due[half:])
                if len(due) == n_f:
                    low = after(low, *tokens_z[1:])
                came = yield swap_f(low, half)
                due = [due[k] + came[k] for k in range(half)]
            part = due[0]
            bias_rows = xor_parts([small[k, images_group * D :] for k in range(n_f)], at_f)
            bias_rows = jnp.stack(bias_rows).astype(f32)
            placed = (bias_rows[:, None, :] * pick_s[None, :, None]).reshape(-1)
            part = (part + placed[: 6 * D]).reshape(-1)
            return act_cols, jnp.concatenate([part, placed[6 * D :]])

        widen_low = widen_weight.astype(bf16).reshape(rows, n_f, n_z, CORES, ub)
        (act_cols, whole), qkv_mine, widen_mine = run(
            modul_chain(),
            trade_seq([qkv_low[:, :, i].reshape(rows, 3 * hd) for i in range(n_s)]),
            trade_mlp(
                [
                    widen_low[:, i // CORES, :, i % CORES].reshape(rows, units)
                    for i in range(n_f * CORES)
                ]
            ),
        )
        qkv_parts = all_f(jnp.stack(qkv_mine))
        qkv_full = jnp.stack(xor_parts(qkv_parts, at_f)).reshape(D, 3 * hd)
        whole = whole + swap_c(whole)
        near = 1
        while near < n_z:
            if 2 * near == n_z:
                whole = after(whole, *qkv_parts[1:])
            whole = whole + swap_z(whole, near)
            near *= 2
        modulation = whole[: images_group * 6 * D].reshape(images_group, 6 * D)
        bias_all = whole[images_group * 6 * D :]
        bias_query = bias_all[:D].reshape(n_s, hd)
        bias_value = bias_all[D : 2 * D].reshape(n_s, hd)
        bias_proj = bias_all[2 * D : 3 * D]
        bias_widen = bias_all[3 * D : 3 * D + FF].reshape(n_f, n_z, CORES, ub)
        bias_narrow = bias_all[3 * D + FF :]

        widen_full = lax.all_gather(jnp.concatenate(widen_mine), "z", axis=0, tiled=False)
        widen_full = widen_full.reshape(n_z, n_f, CORES * rows, units)
        widen_full = widen_full.transpose(1, 0, 2, 3).reshape(D, units)
        narrow_late = after(narrow_weight, *widen_mine).astype(bf16)
        narrow_full = lax.all_gather(narrow_late, "z", axis=0, tiled=True)

        own_id = lax.dynamic_index_in_dim(local_ids, at_s, keepdims=False)
        image_pick = (own_id == jnp.arange(images_group, dtype=jnp.int32)).astype(f32)
        if images_group == 1:
            own_row = modulation[0]
            group_rows = modulation
        else:
            own_row = jnp.sum(image_pick[:, None] * modulation, axis=0)
            rel_ids = xor_take(local_ids, at_s)
            rel_pick = (
                rel_ids[:, None] == jnp.arange(images_group, dtype=jnp.int32)[None, :]
            ).astype(f32)
            group_rows = jnp.sum(rel_pick[:, :, None] * modulation[None, :, :], axis=1)
            arrange = jnp.argsort(rel_ids, stable=True)
            restore = jnp.argsort(arrange, stable=True)
        shift_a, scale_a, gate_a, shift_b, scale_b, gate_b = [
            own_row[i * D : (i + 1) * D] for i in range(6)
        ]

        def in_images(values, order):
            if images_group > 1:
                values = values.reshape(n_s, BLOCK, -1)[order]
            return values.reshape(images_group, SEQ_LEN, -1)

        def send_blocks(values):
            came = swap_c(values[:, 1])
            parts = [swap_z(jnp.stack([values[k, 0], came[k]]), k) for k in range(n_z)]
            pairs = [by_core(part[0], part[1]) for part in xor_parts(parts, at_z)]
            return jnp.concatenate([part for pair in pairs for part in pair], axis=1)

        def send_heads(values):
            parts = [values[:, i * hd : (i + 1) * hd] for i in range(n_s)]
            pairs = [by_core(parts[2 * i], parts[2 * i + 1]) for i in range(n_z)]
            own = xor_parts([pair[0] for pair in pairs], at_z)
            other = xor_parts([pair[1] for pair in pairs], at_z)
            came = swap_c(jnp.stack(other))
            parts = [swap_z(jnp.stack([own[k], came[k]]), k) for k in range(n_z)]
            return jnp.stack(parts).reshape(tok_group, hd)

        grad_out = cotangent.astype(f32)
        d_b_own = (gate_b * grad_out).astype(bf16)

        normed_group, _ = normalize(tokens_group.astype(f32))
        h_a = (
            normed_group * (1.0 + group_rows[:, None, D : 2 * D]) + group_rows[:, None, :D]
        ).astype(bf16)
        h_a = h_a.reshape(tok_group, D)
        query_bias = lax.dynamic_index_in_dim(bias_query, at_s, keepdims=False)
        value_bias = lax.dynamic_index_in_dim(bias_value, at_s, keepdims=False)
        qkv_bias = jnp.concatenate([query_bias, jnp.zeros((hd,), f32), value_bias])
        qkv = (matmul(h_a, qkv_full) + qkv_bias).astype(bf16)
        order = None if images_group == 1 else arrange
        attended = attention(in_images(qkv, order))
        if images_group > 1:
            attended = attended.reshape(n_s, BLOCK, hd)[restore]
        attended = attended.reshape(tok_group, hd)
        attended = after(attended, proj_full)
        att_own = send_blocks(attended.reshape(n_z, CORES, BLOCK, hd))

        branch_a = matmul(att_own, proj_full) + bias_proj
        inputs = tokens.astype(f32)
        middle = inputs + gate_a * branch_a
        normed_b, spread_b = normalize(middle)
        h_b_own = (normed_b * (1.0 + scale_b) + shift_b).astype(bf16)

        d_b_f = after(alone(double(d_b_own, swap_f, n_f)), h_b_own)
        modul_rows = lax.all_gather(after(modul_low, h_b_own), "fsdp", axis=0, tiled=True)
        d_b = with_cores([d_b_f[k] for k in range(n_f)])
        h_b = with_cores(all_f(h_b_own))
        bias_units = lax.dynamic_index_in_dim(bias_widen, at_f, 0, keepdims=False)
        bias_units = lax.dynamic_index_in_dim(bias_units, at_c, 1, keepdims=False).reshape(units)
        widened = matmul(h_b, widen_full) + bias_units
        activated, gelu_pull = jax.vjp(lambda u: jax.nn.gelu(u, approximate=True), widened)
        activated = activated.astype(bf16)
        d_act = jnp.einsum("td,fd->tf", d_b, narrow_full, preferred_element_type=f32)
        d_wide = gelu_pull(d_act)[0].astype(bf16)
        d_hb_part = jnp.einsum("tf,df->td", d_wide, widen_full, preferred_element_type=f32)
        d_hb_f = join_cores(d_hb_part.reshape(n_f, CORES, BLOCK, D))
        d_hb_came = [swap_f(d_hb_f[k].astype(bf16), k) for k in range(1, n_f)]
        grad_narrow = jnp.einsum("tf,td->fd", activated, d_b, preferred_element_type=f32)
        grad_narrow = after(grad_narrow, *d_hb_f).reshape(n_z, ub, D)
        narrow_chain = halve_near(
            [
                lax.dynamic_index_in_dim(grad_narrow, at_z ^ k, 0, keepdims=False)
                for k in range(n_z)
            ],
            swap_z,
        )
        narrow_came = next(narrow_chain)
        d_hb = add_parts(d_hb_f[0], [after(part, narrow_came) for part in d_hb_came])
        branch_part = matmul(activated, narrow_full).reshape(n_f, CORES, BLOCK, D)
        grad_widen = jnp.einsum("td,tf->df", h_b, d_wide, preferred_element_type=f32)
        grad_widen = grad_widen.astype(bf16).reshape(n_f, n_z, CORES, rows, units)
        grad_widen = grad_widen.transpose(1, 0, 2, 3, 4).reshape(n_z, -1, units)

        d_shift_b = jnp.sum(d_hb, axis=0)
        d_scale_b = jnp.sum(d_hb * normed_b, axis=0)
        d_middle = grad_out + norm_back(d_hb * (1.0 + scale_b), normed_b, spread_b)
        d_gate_a = jnp.sum(d_middle * branch_a, axis=0)
        d_a = (gate_a * d_middle).astype(bf16)
        d_att_own = jnp.einsum("te,de->td", d_a, proj_full, preferred_element_type=f32)
        d_att_own = d_att_own.astype(bf16)
        d_att = send_heads(d_att_own)
        branch_chain = halve(join_cores(after(branch_part, d_hb)), swap_f)
        branch_came = next(branch_chain)

        def further(chain, came):
            try:
                return chain.send(came), None
            except StopIteration as stop:
                return None, stop.value

        narrow_came, narrow_sum = further(narrow_chain, narrow_came)
        if narrow_came is not None:
            d_att, narrow_came, branch_came = lax.optimization_barrier(
                (d_att, narrow_came, branch_came)
            )
        else:
            d_att, branch_came = lax.optimization_barrier((d_att, branch_came))
        branch_came, branch_b = further(branch_chain, branch_came)
        grad_widen = after(grad_widen, d_att)
        widen_part = lax.psum_scatter(grad_widen, "z", scatter_dimension=0, tiled=False)

        d_qkv = attention_grads(in_images(qkv, order), in_images(d_att, order))
        if images_group > 1:
            d_qkv = d_qkv.reshape(n_s, BLOCK, 3 * hd)[restore]
        d_qkv = d_qkv.reshape(tok_group, 3 * hd)
        if branch_came is not None:
            d_qkv, branch_came = lax.optimization_barrier((d_qkv, branch_came))
        grad_proj = jnp.einsum(
            "td,te->de", att_own, after(d_a, d_qkv), preferred_element_type=f32
        )
        grad_proj = grad_proj.reshape(n_f, n_z, CORES, rows, D)
        proj_own, proj_other = by_core(grad_proj[:, :, 0], grad_proj[:, :, 1])
        proj_both = proj_own + swap_c(proj_other.astype(bf16)).astype(f32)
        proj_chain = halve(
            [
                lax.dynamic_index_in_dim(proj_both, at_f ^ k, 0, keepdims=False)
                for k in range(n_f)
            ],
            swap_f,
        )
        d_ha_part = jnp.einsum("te,de->td", d_qkv, qkv_full, preferred_element_type=f32)
        d_ha_z = join_cores(d_ha_part.reshape(n_z, CORES, BLOCK, D))
        d_ha_low = [d_ha_z[k].astype(bf16) for k in range(1, n_z)]
        d_ha_came = [swap_z(d_ha_low[k - 1], k) for k in range(1, n_z)]
        grad_qkv = jnp.einsum("td,te->de", after(h_a, d_ha_part), d_qkv, preferred_element_type=f32)
        grad_qkv = after(grad_qkv.reshape(n_f, n_s * rows, 3 * hd), *d_ha_low)
        grad_qkv = [
            lax.dynamic_index_in_dim(grad_qkv, at_f ^ k, 0, keepdims=False) for k in range(n_f)
        ]
        widen_part = after(widen_part, *d_ha_low).reshape(n_f * CORES, rows, units)

        if branch_came is not None:
            branch_b = alone(resume(branch_chain, branch_came))
        if narrow_came is not None:
            narrow_sum = alone(resume(narrow_chain, narrow_came))
        proj_came = next(proj_chain)
        qkv_chain = halve(grad_qkv, swap_f)
        qkv_came = next(qkv_chain)
        widen_chain = trade_mlp([widen_part[i] for i in range(n_f * CORES)])
        widen_came = next(widen_chain)
        d_ha = add_parts(d_ha_z[0], d_ha_came)
        branch_b = branch_b + bias_narrow
        block_output = (middle + gate_b * branch_b).astype(bf16)
        d_gate_b = jnp.sum(grad_out * branch_b, axis=0)
        normed_a, spread_a = normalize(inputs)
        d_shift_a = jnp.sum(d_ha, axis=0)
        d_scale_a = jnp.sum(d_ha * normed_a, axis=0)
        tokens_grad = (
            d_middle + norm_back(d_ha * (1.0 + scale_a), normed_a, spread_a)
        ).astype(bf16)

        units_sum = column_sums(d_wide).reshape(n_z, ub)
        bias_g_widen = (
            pick_f[:, None, None, None] * pick_c[None, None, :, None] * units_sum[None, :, None, :]
        ).reshape(FF)
        heads_sum = column_sums(d_qkv)
        bias_g_query = (pick_s[:, None] * heads_sum[None, :hd]).reshape(D)
        bias_g_value = (pick_s[:, None] * heads_sum[None, 2 * hd :]).reshape(D)
        d_block = jnp.concatenate([d_shift_a, d_scale_a, d_gate_a, d_shift_b, d_scale_b, d_gate_b])
        per_image = (image_pick[:, None] * d_block[None, :]).reshape(-1)
        pieces = [
            per_image,
            bias_g_query,
            bias_g_value,
            column_sums(d_a),
            bias_g_widen,
            column_sums(d_b_own),
        ]
        sums = alone(add_seq(jnp.concatenate(pieces)))
        cut = images_group * 6 * D
        d_own = sums[:cut].reshape(images_group, 6 * D)
        d_cond_rows = jnp.einsum(
            "im,dm->id",
            d_own,
            modul_rows.astype(f32),
            precision=lax.Precision.HIGHEST,
            preferred_element_type=f32,
        )

        def cond_chain():
            part = yield from double(d_cond_rows, swap_z, n_z)
            part = jnp.stack(xor_parts([part[k] for k in range(n_z)], at_z))
            came = yield swap_c(part)
            return jnp.stack(by_core(part, came), axis=1)

        def proj_rest():
            mid = yield from resume(proj_chain, proj_came)
            mid = xor_parts([mid[k] for k in range(n_z)], at_z)
            return (yield from halve(mid, swap_z))

        def qkv_rest():
            mid = yield from resume(qkv_chain, qkv_came)
            return (yield from trade_seq([mid[i : i + rows] for i in range(0, n_s * rows, rows)]))

        whole, d_cond, proj_sum, qkv_sum, widen_back = run(
            double(sums, swap_f, n_f),
            cond_chain(),
            proj_rest(),
            qkv_rest(),
            resume(widen_chain, widen_came),
        )
        widen_sum = jnp.stack(widen_back).reshape(n_f, CORES, rows, n_z, ub)
        widen_sum = widen_sum.transpose(2, 0, 3, 1, 4).reshape(rows, FF).astype(f32)
        qkv_sum = jnp.stack(qkv_sum).reshape(n_s, rows, 3, hd)
        qkv_sum = qkv_sum.transpose(1, 2, 0, 3).reshape(rows, 3 * D)
        d_cond = d_cond.reshape(n_s, images_group, n_f, rows)
        d_cond_act = d_cond.transpose(1, 2, 0, 3).reshape(images_group, D)
        silu_pull = jax.vjp(jax.nn.silu, cond_float)[1]
        condition_grad = silu_pull(d_cond_act)[0]

        d_modulation = whole[:, :cut].reshape(n_f * images_group, 6 * D)
        act_wide = act_cols.astype(f32)
        modul_sum = sum(
            act_wide[i][:, None] * d_modulation[i][None, :] for i in range(n_f * images_group)
        )
        bias_grad = jnp.concatenate(
            [jnp.sum(d_modulation, axis=0), jnp.sum(whole[:, cut:], axis=0)]
        )
        bias_sum = lax.dynamic_slice_in_dim(bias_grad, at_g * width, width)

        rate_wide = 2.0 / math.sqrt(D)
        modul_new = adam_step(modul_weight, modul_sum, modul_mean, modul_square, rate_wide)
        qkv_new = adam_step(qkv_weight, qkv_sum, qkv_mean, qkv_square, rate_wide)
        proj_new = adam_step(
            proj_weight, proj_sum, proj_mean, proj_square, 2.0 / math.sqrt(D // 16)
        )
        widen_new = adam_step(widen_weight, widen_sum, widen_mean, widen_square, rate_wide)
        narrow_new = adam_step(
            narrow_weight, narrow_sum, narrow_mean, narrow_square, 2.0 / math.sqrt(FF)
        )
        bias_new = adam_step(bias_vector, bias_sum, bias_mean, bias_square, 0.5)
        news = (modul_new, qkv_new, proj_new, widen_new, narrow_new, bias_new)
        return (
            block_output,
            tokens_grad,
            condition_grad,
            *[new[0] for new in news],
            *[new[1] for new in news],
            *[new[2] for new in news],
        )

    return shards


def solution(mesh):
    n_f, n_s = mesh.shape["fsdp"], mesh.shape["seq"]
    n_z = n_s // CORES
    cores = jax.sharding.Mesh(mesh.devices.reshape(n_f, n_z, CORES), ("fsdp", "z", "core"))
    both = P(("fsdp", "z", "core"), None)
    flat = P(("fsdp", "z", "core"))
    params = (both, both, both, both, both, flat)
    return jax.shard_map(
        make_shards(n_f, n_z),
        mesh=cores,
        in_specs=(both, P("fsdp", None), P("fsdp"), both) + params * 3,
        out_specs=(both, both, P("fsdp", None)) + params * 3,
        check_vma=False,
    )
```
